256 devices in a mesh: dp: 8 (over x, z_lo), ctx: 32 (over z_hi, y, core).
Axes of the slice: x: 4, y: 4, z: 8 (z_hi: 4, z_lo: 2; z = z_hi * 2 + z_lo), core: 2. Of those that a mesh axis runs over, the one named last changes fastest.
Arguments:
- streams: bfloat16 [3, 32768, 4096], P(None, ('dp', 'ctx')), may hold values from -6 to 6
- out_grad: bfloat16 [32768, 4096], P(('dp', 'ctx')), may hold values from -6 to 6
- proj_weight: bfloat16 [4096, 4096], P('dp'), may hold values from -0.09375 to 0.09375
- long_filter: float32 [4096, 4096], P('dp', 'ctx'), may hold values from -0.09375 to 0.09375
- short_taps: float32 [3, 3, 4096], replicated, may hold values from -3 to 3
- doc_ids: int32 [32768], replicated, may hold values from 0 to 127, never falling along the last dimension, each value on 1 to 1024 neighbouring positions
Outputs:
- stream_grads: bfloat16 [3, 32768, 4096], P(None, ('dp', 'ctx'))
- proj_grad: float32 [4096, 4096], P(('dp', 'ctx'))
- filter_grad: float32 [4096, 4096], P('dp', 'ctx')
- tap_grad: float32 [3, 3, 4096], replicated
The draws below stay inside these ranges and needn't reach their ends.
Inputs may be any that keep to these rules, and one draw needn't show every extreme that they name: `doc_ids`: never falls along the tokens; documents hold 1 to 1024 tokens and may cross device and sequence ends.
All inputs are finite; a program needn't handle non-finite values.
Results may differ from the reference program's by a relative error of at most 0.024.
Values may be sent and summed in bfloat16 or wider, within the bound.
A program may use at most 192 MiB of HBM per device.

```python
import math
import jax
import jax.numpy as jnp
import numpy as np
from jax import lax

CHANNELS = 4096
FEATURES = 4096
TAPS = 3
WINDOW = 4096
TOKENS = 32768
N_DP = 8


def steps_of(stream_key, dims, shards, least, high):
    factor_of = 1.0
    for axis_at, parts in shards:
        heights = jax.random.uniform(jax.random.fold_in(jax.random.fold_in(stream_key, 6), axis_at), (parts,), jnp.float32, least / len(shards), high / len(shards))
        factor_of = factor_of * jnp.repeat(jnp.exp(heights), dims[axis_at] // parts).reshape((-1,) + (1,) * (len(dims) - 1 - axis_at))
    return factor_of


def length_profile(number_of, total, most, skew):
    loads = [(1 << 20) // math.isqrt(rank ** skew) + 1 for rank in range(2, number_of + 1)]
    rest, holding = total - most - (number_of - 1), [1] * (number_of - 1)
    while rest > 0:
        free = [i for i in range(number_of - 1) if holding[i] < most]
        whole, remaining = sum([loads[i] for i in free]), rest
        for i in free:
            extra = min(most - holding[i], max(1, remaining * loads[i] // whole), rest)
            holding[i] = holding[i] + extra
            rest = rest - extra
    return np.array([most] + holding)


def uneven_parts(stream_key, number_of, total, limit, slope):
    if number_of == 2:
        one = jax.random.randint(stream_key, (), max(1, total - limit), min(limit, total - 1) + 1)
        return jnp.stack([one, total - one])
    tallies = jnp.asarray(length_profile(number_of, total, limit, slope), jnp.int32)
    pairs = (number_of - 1) // 2
    giver, taker = tallies[1:1 + 2 * pairs:2], tallies[2:2 + 2 * pairs:2]
    slack = jnp.minimum(giver - 1, limit - taker)
    moved = jax.random.randint(jax.random.fold_in(stream_key, 1), (pairs,), 0, 1 << 20) % (slack + 1)
    tallies = tallies.at[1:1 + 2 * pairs:2].set(giver - moved).at[2:2 + 2 * pairs:2].set(taker + moved)
    return tallies[jax.random.permutation(jax.random.fold_in(stream_key, 2), number_of)]


def centred(rng, extent, spread, bound, split=(), kind=jnp.bfloat16):
    level = steps_of(rng, extent, split, -0.22, 0.18) if split else 1.0
    drawn = jax.random.normal(rng, extent, jnp.float32) * spread * level
    return jnp.minimum(jnp.maximum(drawn, -bound), bound).astype(kind)


def setup_inputs(seed: int = 0) -> dict:
    keys = jax.random.split(jax.random.key(seed), 7)
    streams = centred(keys[0], (3, TOKENS, CHANNELS), 1.0, 6.0, ((1, 256),))
    out_grad = centred(keys[1], (TOKENS, FEATURES), 1.0, 6.0, ((0, 256),))
    proj_weight = centred(keys[2], (CHANNELS, FEATURES), CHANNELS ** -0.5, 0.09375, ((0, 8),))
    long_filter = centred(keys[3], (WINDOW, CHANNELS), WINDOW ** -0.5, 0.09375, ((0, 8), (1, 32)), jnp.float32)
    short_taps = centred(keys[4], (TAPS, 3, CHANNELS), 0.6, 3.0, (), jnp.float32)
    doc_ids = jnp.searchsorted(jnp.cumsum(uneven_parts(keys[5], max(4, TOKENS // 256), TOKENS, min(1024, TOKENS // 2), 2)), jnp.arange(TOKENS), side="right").astype(jnp.int32)
    return {"streams": streams, "out_grad": out_grad, "proj_weight": proj_weight, "long_filter": long_filter, "short_taps": short_taps, "doc_ids": doc_ids}


def causal_filter(signal, kernel):
    length = signal.shape[0]
    spectrum = jnp.fft.rfft(signal, 2 * length, axis=0) * jnp.fft.rfft(kernel, 2 * length, axis=0)
    return jnp.fft.irfft(spectrum, 2 * length, axis=0)[:length]


def reverse_filter(signal, kernel):
    length = signal.shape[0]
    spectrum = jnp.conj(jnp.fft.rfft(kernel, 2 * length, axis=0)) * jnp.fft.rfft(signal, 2 * length, axis=0)
    return jnp.fft.irfft(spectrum, 2 * length, axis=0)[:length]


def delay_rows(values, offset):
    if offset == 0:
        return values
    blank = jnp.zeros((values.shape[0], offset, values.shape[2]), values.dtype)
    return jnp.concatenate([blank, values[:, :values.shape[1] - offset]], axis=1)


def advance_rows(values, offset):
    if offset == 0:
        return values
    blank = jnp.zeros((values.shape[0], offset, values.shape[2]), values.dtype)
    return jnp.concatenate([values[:, offset:], blank], axis=1)


def delay_ids(ids, offset):
    if offset == 0:
        return ids
    return jnp.concatenate([jnp.full((offset,), -1, jnp.int32), ids[:ids.shape[0] - offset]])


def advance_ids(ids, offset):
    if offset == 0:
        return ids
    return jnp.concatenate([ids[offset:], jnp.full((offset,), -1, jnp.int32)])


def reference(streams, out_grad, proj_weight, long_filter, short_taps, doc_ids):
    grad_scale = TOKENS ** -0.5
    stream_groups = streams.reshape(3, N_DP, WINDOW, CHANNELS).transpose(1, 0, 2, 3)
    grad_groups = out_grad.reshape(N_DP, WINDOW, FEATURES)
    id_groups = doc_ids.reshape(N_DP, WINDOW)

    def group_step(totals, item):
        weight_total, filter_total, tap_total = totals
        stream_rows, grad_rows, id_rows = item
        values = stream_rows.astype(jnp.float32)
        conv_out = jnp.zeros(values.shape, jnp.float32)
        for offset in range(TAPS):
            same_doc = (delay_ids(id_rows, offset) == id_rows).astype(jnp.float32)
            conv_out = conv_out + short_taps[offset][:, None, :] * delay_rows(values, offset) * same_doc[None, :, None]
        query = conv_out[0].astype(jnp.bfloat16)
        key_stream = conv_out[1]
        value_stream = conv_out[2]
        product = (key_stream * value_stream).astype(jnp.bfloat16)
        filtered = causal_filter(product.astype(jnp.float32), long_filter).astype(jnp.bfloat16)
        mixed = (query.astype(jnp.float32) * filtered.astype(jnp.float32)).astype(jnp.bfloat16)
        mix_grad = lax.dot_general(grad_rows, proj_weight, (((1,), (1,)), ((), ())),
                                   preferred_element_type=jnp.float32).astype(jnp.bfloat16)
        weight_term = lax.dot_general(mixed, grad_rows, (((0,), (0,)), ((), ())),
                                      preferred_element_type=jnp.float32)
        query_grad = (mix_grad.astype(jnp.float32) * filtered.astype(jnp.float32)).astype(jnp.bfloat16)
        filtered_grad = (mix_grad.astype(jnp.float32) * query.astype(jnp.float32)).astype(jnp.bfloat16)
        product_grad = reverse_filter(filtered_grad.astype(jnp.float32), long_filter).astype(jnp.bfloat16)
        filter_term = reverse_filter(filtered_grad.astype(jnp.float32), product.astype(jnp.float32))
        conv_grad = jnp.stack([query_grad.astype(jnp.float32),
                               product_grad.astype(jnp.float32) * value_stream,
                               product_grad.astype(jnp.float32) * key_stream])
        stream_grad = jnp.zeros(values.shape, jnp.float32)
        tap_terms = []
        for offset in range(TAPS):
            ahead_same = (advance_ids(id_rows, offset) == id_rows).astype(jnp.float32)
            stream_grad = stream_grad + short_taps[offset][:, None, :] * advance_rows(conv_grad, offset) * ahead_same[None, :, None]
            behind_same = (delay_ids(id_rows, offset) == id_rows).astype(jnp.float32)
            tap_terms.append(jnp.sum(conv_grad * delay_rows(values, offset) * behind_same[None, :, None], axis=1))
        totals = (weight_total + weight_term, filter_total + filter_term, tap_total + jnp.stack(tap_terms))
        return totals, stream_grad.astype(jnp.bfloat16)

    start = (jnp.zeros((CHANNELS, FEATURES), jnp.float32), jnp.zeros((WINDOW, CHANNELS), jnp.float32),
             jnp.zeros((TAPS, 3, CHANNELS), jnp.float32))
    totals, grads = lax.scan(group_step, start, (stream_groups, grad_groups, id_groups))
    stream_grads = grads.transpose(1, 0, 2, 3).reshape(3, TOKENS, CHANNELS)
    return stream_grads, totals[0] * grad_scale, totals[1] * grad_scale, totals[2] * grad_scale
```

```python
import functools
import math

import jax
import jax.numpy as jnp
import numpy as np
from jax import lax
from jax.experimental import pallas as pl
from jax.experimental.pallas import tpu as pltpu
from jax.sharding import Mesh
from jax.sharding import PartitionSpec as P

DP = ("x", "w")
CTX = ("z", "y", "c")
F32 = jnp.float32
BF16 = jnp.bfloat16
LENGTH = 4096
TOTAL = 2 * LENGTH
SLOTS = 32
STEP = 128
WIDE = 512
GRAD_SCALE = float(32768) ** (-0.5)
MESH = pl.DeviceIdType.MESH


def split_table(table):
    return table.astype(BF16)


def make_tables():
    a = np.arange(32)
    b = np.arange(STEP)
    first = np.zeros((2 * SLOTS, 32))
    first[0] = 1.0
    first[1] = (-1.0) ** a
    for s in range(1, SLOTS):
        first[2 * s] = np.cos(2 * np.pi * a * s / 64)
        first[2 * s + 1] = -np.sin(2 * np.pi * a * s / 64)
    first_wide = np.kron(first, np.eye(8))
    last_wide = np.kron(first.T * (2.0 / TOTAL), np.eye(8))
    angle = 2 * np.pi * np.outer(b, b) / STEP
    cosine, sine = np.cos(angle), np.sin(angle)
    plain = np.block([[cosine, sine], [-sine, cosine]])
    special = np.zeros((2 * STEP, 2 * STEP))
    half = np.arange(64)
    even = 2 * np.pi * np.outer(half, b) / STEP
    odd = 2 * np.pi * np.outer(32 + 64 * half, b) / TOTAL
    special[:64, :STEP] = np.cos(even)
    special[64:128, STEP:] = np.cos(odd)
    special[128:192, :STEP] = -np.sin(even)
    special[128, :STEP] = (-1.0) ** b
    special[192:, STEP:] = -np.sin(odd)
    middle = np.stack([split_table(special), split_table(plain)])
    middle_back = np.stack([split_table(special.T), split_table(plain.T)])
    turn = 2 * np.pi * np.outer(np.arange(SLOTS), b) / TOTAL
    twist = np.concatenate([np.cos(turn), np.sin(turn)], 1).astype(np.float32)
    return split_table(first_wide), split_table(last_wide), middle, middle_back, twist


def dot32(a, b):
    return jnp.dot(a, b, preferred_element_type=F32)


def dot16(table, value):
    return dot32(table, value.astype(BF16))


def twisted(re, im, c, s):
    return re * c + im * s, im * c - re * s


def untwisted(re, im, c, s):
    return re * c - im * s, im * c + re * s


def halves_of(block):
    return [block[:, :8, :].reshape(256, STEP), block[:, 8:, :].reshape(256, STEP)]


def edge_rows(k):
    rows = lax.broadcasted_iota(jnp.int32, (STEP, STEP), 0)
    return jnp.logical_and(rows == 0, k == 0)


def filter_forward_kernel(
    prod_ref, filt_ref, first_ref, last_ref, mid_ref, back_ref, twist_ref,
    out_ref, spec_prod_ref, spec_filt_ref, yp_ref, yf_ref,
):
    first = first_ref[...]

    @pl.loop(0, 8, unroll=2)
    def _(h):
        rows = pl.ds(pl.multiple_of(16 * h, 16), 16)
        prods = halves_of(prod_ref[:, rows, :].astype(F32))
        filts = halves_of(filt_ref[:, rows, :].astype(F32))
        for j in range(2):
            wide = dot32(first, jnp.concatenate([prods[j], filts[j]], 1).astype(BF16))
            at = pl.ds(pl.multiple_of(16 * h + 8 * j, 8), 8)
            yp_ref[:, at, :] = wide[:, :128].reshape(64, 8, STEP)
            yf_ref[:, at, :] = wide[:, 128:].reshape(64, 8, STEP)

    @pl.loop(0, SLOTS, unroll=4)
    def _(k):
        c, s = twist_ref[k, :STEP, :], twist_ref[k, STEP:, :]
        which = jnp.minimum(k, 1)
        pair = pl.ds(2 * k, 2)
        yp, yf = yp_ref[pair], yf_ref[pair]
        pr, pi = twisted(yp[0], yp[1], c, s)
        fr, fi = twisted(yf[0], yf[1], c, s)
        value = jnp.concatenate([jnp.concatenate([pr, pi], 0), jnp.concatenate([fr, fi], 0)], 1)
        spec = dot16(mid_ref[which], value)
        spec_prod_ref[k] = spec[:, :128]
        spec_filt_ref[k] = spec[:, 128:]
        pr, pi = spec[:128, :128], spec[128:, :128]
        fr, fi = spec[:128, 128:], spec[128:, 128:]
        edge = edge_rows(k)
        re = jnp.where(edge, 0.5 * (pr * fr), pr * fr - pi * fi)
        im = jnp.where(edge, 0.5 * (pi * fi), pr * fi + pi * fr)
        back = dot16(back_ref[which], jnp.concatenate([re, im], 0))
        re, im = untwisted(back[:128], back[128:], c, s)
        yp_ref[2 * k] = re
        yp_ref[2 * k + 1] = im

    last = last_ref[...]

    @pl.loop(0, 8, unroll=2)
    def _(h):
        halves = [yp_ref[:, pl.ds(pl.multiple_of(16 * h + 8 * j, 8), 8), :].reshape(512, STEP) for j in range(2)]
        out = dot16(last, jnp.concatenate(halves, 1))
        parts = [out[:, 128 * j : 128 * (j + 1)].reshape(32, 8, STEP) for j in range(2)]
        rows = pl.ds(pl.multiple_of(16 * h, 16), 16)
        out_ref[:, rows, :] = jnp.concatenate(parts, 1).astype(BF16)


def filter_backward_kernel(
    grad_ref, spec_prod_ref, spec_filt_ref, first_ref, last_ref, mid_ref, back_ref, twist_ref,
    prod_grad_ref, filt_grad_ref, yg_ref, yv_ref,
):
    first = first_ref[...]

    @pl.loop(0, 8, unroll=2)
    def _(h):
        rows = pl.ds(pl.multiple_of(16 * h, 16), 16)
        grads = halves_of(grad_ref[:, rows, :].astype(F32))
        grad = jnp.concatenate([grads[0], grads[1]], 1).astype(BF16)
        out = dot32(first, grad)
        for j in range(2):
            at = pl.ds(pl.multiple_of(16 * h + 8 * j, 8), 8)
            yg_ref[:, at, :] = out[:, 128 * j : 128 * (j + 1)].reshape(64, 8, STEP)

    @pl.loop(0, SLOTS, unroll=4)
    def _(k):
        c, s = twist_ref[k, :STEP, :], twist_ref[k, STEP:, :]
        which = jnp.minimum(k, 1)
        yg = yg_ref[pl.ds(2 * k, 2)]
        gr, gi = twisted(yg[0], yg[1], c, s)
        spec = dot16(mid_ref[which], jnp.concatenate([gr, gi], 0))
        gr, gi = spec[:128], spec[128:]
        edge = edge_rows(k)
        cols = []
        for ref in (spec_filt_ref, spec_prod_ref):
            hr, hi = ref[k, :STEP, :], ref[k, STEP:, :]
            re = jnp.where(edge, 0.5 * (hr * gr), hr * gr + hi * gi)
            im = jnp.where(edge, 0.5 * (hi * gi), hr * gi - hi * gr)
            cols.append(jnp.concatenate([re, im], 0))
        back = dot16(back_ref[which], jnp.concatenate(cols, 1))
        re, im = untwisted(back[:128, :128], back[128:, :128], c, s)
        yg_ref[2 * k] = re
        yg_ref[2 * k + 1] = im
        re, im = untwisted(back[:128, 128:], back[128:, 128:], c, s)
        yv_ref[2 * k] = re
        yv_ref[2 * k + 1] = im

    last = last_ref[...]

    @pl.loop(0, 8, unroll=2)
    def _(h):
        parts, other = [], []
        for j in range(2):
            at = pl.ds(pl.multiple_of(16 * h + 8 * j, 8), 8)
            value = jnp.concatenate([yg_ref[:, at, :].reshape(512, STEP), yv_ref[:, at, :].reshape(512, STEP)], 1)
            out = dot16(last, value)
            parts.append(out[:, :128].reshape(32, 8, STEP))
            other.append(out[:, 128:].reshape(32, 8, STEP))
        rows = pl.ds(pl.multiple_of(16 * h, 16), 16)
        prod_grad_ref[:, rows, :] = jnp.concatenate(parts, 1).astype(BF16)
        filt_grad_ref[:, rows, :] = jnp.concatenate(other, 1).astype(BF16)


def vmem():
    return pl.BlockSpec(memory_space=pltpu.VMEM)


def tables_in():
    first, last, middle, back, twist = make_tables()
    wide = jnp.broadcast_to(jnp.asarray(twist)[:, :, None], (SLOTS, 2 * STEP, STEP))
    return [jnp.asarray(first), jnp.asarray(last), jnp.asarray(middle), jnp.asarray(back), wide]


def filter_forward(prod, filt, tables):
    spec = jax.ShapeDtypeStruct((SLOTS, 2 * STEP, STEP), F32)
    return pl.pallas_call(
        filter_forward_kernel,
        out_shape=[jax.ShapeDtypeStruct((32, STEP, STEP), BF16), spec, spec],
        in_specs=[vmem()] * 7,
        out_specs=[vmem()] * 3,
        scratch_shapes=[pltpu.VMEM((64, STEP, STEP), F32)] * 2,
        compiler_params=pltpu.CompilerParams(vmem_limit_bytes=40 * 1024 * 1024),
        cost_estimate=pl.CostEstimate(flops=12 * 10**9, bytes_accessed=18 * 2**20, transcendentals=0),
        name="filter_forward",
    )(prod, filt, *tables)


def filter_backward(grad, spec_prod, spec_filt, tables):
    out = jax.ShapeDtypeStruct((32, STEP, STEP), BF16)
    return pl.pallas_call(
        filter_backward_kernel,
        out_shape=[out, out],
        in_specs=[vmem()] * 8,
        out_specs=[vmem()] * 2,
        scratch_shapes=[pltpu.VMEM((64, STEP, STEP), F32)] * 2,
        compiler_params=pltpu.CompilerParams(vmem_limit_bytes=40 * 1024 * 1024),
        cost_estimate=pl.CostEstimate(flops=12 * 10**9, bytes_accessed=18 * 2**20, transcendentals=0),
        name="filter_backward",
    )(grad, spec_prod, spec_filt, *tables)


def convolved(ext_ref, taps_ref, masks, stream):
    total = taps_ref[0, stream : stream + 1, :] * ext_ref[stream, pl.ds(8, STEP), :]
    for i in (1, 2):
        total = total + taps_ref[i, stream : stream + 1, :] * ext_ref[stream, pl.ds(8 - i, STEP), :] * masks[i - 1]
    return total


def fill_extended(streams_ref, early_ref, ext_ref):
    for s in range(3):
        ext_ref[s, pl.ds(6, 2), :] = early_ref[s].astype(F32)
        ext_ref[s, pl.ds(8, STEP), :] = streams_ref[s].astype(F32)


def short_kernel(streams_ref, early_ref, taps_ref, masks_ref, query_ref, prod_ref, head_ref, ext_ref):
    fill_extended(streams_ref, early_ref, ext_ref)
    masks = [masks_ref[:, i : i + 1] for i in range(2)]
    query_ref[...] = convolved(ext_ref, taps_ref, masks, 0).astype(BF16)
    key = convolved(ext_ref, taps_ref, masks, 1)
    value = convolved(ext_ref, taps_ref, masks, 2)
    head_ref[0] = key[:8]
    head_ref[1] = value[:8]
    prod = (key * value).astype(BF16)
    for j in range(4):
        prod_ref[j] = prod[:, 128 * j : 128 * (j + 1)]


def rows_spec(lead, rows):
    return pl.BlockSpec((lead, rows, WIDE), lambda i: (0, 0, i))


def flat_spec(rows):
    return pl.BlockSpec((rows, WIDE), lambda i: (0, i))


def chan_spec(rows=STEP):
    return pl.BlockSpec((4, rows, STEP), lambda i: (i, 0, 0))


def slab_spec(rows=STEP):
    return pl.BlockSpec((1, rows, WIDE), lambda i: (i, 0, 0))


def pair_spec(rows=STEP):
    return pl.BlockSpec((1, rows, WIDE), lambda i: (i // 2, 0, i % 2))


def mask_spec():
    return pl.BlockSpec((STEP, 8), lambda i: (0, 0))


def short_filter(streams, early, taps, masks):
    return pl.pallas_call(
        short_kernel,
        grid=(8,),
        out_shape=[
            jax.ShapeDtypeStruct((STEP, 4096), BF16),
            jax.ShapeDtypeStruct((32, STEP, STEP), BF16),
            jax.ShapeDtypeStruct((2, 8, 4096), F32),
        ],
        in_specs=[rows_spec(3, STEP), rows_spec(3, 2), rows_spec(3, 3), mask_spec()],
        out_specs=[flat_spec(STEP), chan_spec(), rows_spec(2, 8)],
        scratch_shapes=[pltpu.VMEM((3, STEP + 8, WIDE), F32)],
        cost_estimate=pl.CostEstimate(flops=10**7, bytes_accessed=5 * 2**20, transcendentals=0),
        name="short_filter",
    )(streams, early, taps, masks)


def mixed_kernel(query_ref, filtered_ref, out_ref):
    filtered = jnp.concatenate([filtered_ref[j] for j in range(4)], 1)
    out_ref[0] = (query_ref[...].astype(F32) * filtered.astype(F32)).astype(BF16)


def mixed_of(query, filtered):
    return pl.pallas_call(
        mixed_kernel,
        grid=(8,),
        out_shape=jax.ShapeDtypeStruct((8, STEP, WIDE), BF16),
        in_specs=[flat_spec(STEP), chan_spec()],
        out_specs=slab_spec(),
        cost_estimate=pl.CostEstimate(flops=10**6, bytes_accessed=3 * 2**20, transcendentals=0),
        name="mixed",
    )(query, filtered)


def filtered_grad_kernel(mix_grad_ref, query_ref, out_ref):
    out = (mix_grad_ref[0].astype(F32) * query_ref[...].astype(F32)).astype(BF16)
    for j in range(4):
        out_ref[j] = out[:, 128 * j : 128 * (j + 1)]


def filtered_grad_of(mix_grad, query):
    return pl.pallas_call(
        filtered_grad_kernel,
        grid=(8,),
        out_shape=jax.ShapeDtypeStruct((32, STEP, STEP), BF16),
        in_specs=[pair_spec(), flat_spec(STEP)],
        out_specs=chan_spec(),
        cost_estimate=pl.CostEstimate(flops=10**6, bytes_accessed=3 * 2**20, transcendentals=0),
        name="filtered_grad",
    )(mix_grad, query)


def lanes_of(ref):
    return jnp.concatenate([ref[j] for j in range(4)], 1)


def final_kernel(
    streams_ref, early_ref, taps_ref, masks_ref, mix_grad_ref, filtered_ref, prod_grad_ref,
    mix_next_ref, filtered_next_ref, prod_next_ref, head_next_ref,
    grads_ref, tap_ref, ext_ref, conv_ref,
):
    fill_extended(streams_ref, early_ref, ext_ref)
    behind = [masks_ref[:, i : i + 1] for i in range(2)]
    ahead = [masks_ref[:, 2 + i : 3 + i] for i in range(2)]
    key = convolved(ext_ref, taps_ref, behind, 1)
    value = convolved(ext_ref, taps_ref, behind, 2)
    prod_grad = lanes_of(prod_grad_ref).astype(F32)
    prod_next = lanes_of(prod_next_ref).astype(F32)[:2]
    body = pl.ds(0, STEP)
    tail = pl.ds(STEP, 2)
    query_grad = mix_grad_ref[0].astype(F32) * lanes_of(filtered_ref).astype(F32)
    conv_ref[0, body, :] = query_grad.astype(BF16).astype(F32)
    query_next = mix_next_ref[0].astype(F32) * lanes_of(filtered_next_ref).astype(F32)
    conv_ref[0, tail, :] = query_next.astype(BF16).astype(F32)[:2]
    conv_ref[1, body, :] = prod_grad * value
    conv_ref[1, tail, :] = prod_next * head_next_ref[1, :2, :]
    conv_ref[2, body, :] = prod_grad * key
    conv_ref[2, tail, :] = prod_next * head_next_ref[0, :2, :]
    for s in range(3):
        here = conv_ref[s, body, :]
        grad = taps_ref[0, s : s + 1, :] * here
        sums = [jnp.sum(here * ext_ref[s, pl.ds(8, STEP), :], axis=0, keepdims=True)]
        for i in (1, 2):
            grad = grad + taps_ref[i, s : s + 1, :] * conv_ref[s, pl.ds(i, STEP), :] * ahead[i - 1]
            behind_rows = ext_ref[s, pl.ds(8 - i, STEP), :] * behind[i - 1]
            sums.append(jnp.sum(here * behind_rows, axis=0, keepdims=True))
        grads_ref[s] = grad.astype(BF16)
        for i in range(3):
            for j in range(4):
                tap_ref[j, 3 * i + s : 3 * i + s + 1, :] = sums[i][:, 128 * j : 128 * (j + 1)]
    for j in range(4):
        tap_ref[j, 9:16, :] = jnp.zeros((7, STEP), F32)


def final_grads(streams, early, taps, masks, mix_grad, filtered, prod_grad, nexts):
    return pl.pallas_call(
        final_kernel,
        grid=(8,),
        out_shape=[
            jax.ShapeDtypeStruct((3, STEP, 4096), BF16),
            jax.ShapeDtypeStruct((32, 16, STEP), F32),
        ],
        in_specs=[
            rows_spec(3, STEP), rows_spec(3, 2), rows_spec(3, 3), mask_spec(),
            pair_spec(), chan_spec(), chan_spec(), pair_spec(16), chan_spec(16), chan_spec(16), rows_spec(2, 8),
        ],
        out_specs=[rows_spec(3, STEP), chan_spec(16)],
        scratch_shapes=[pltpu.VMEM((3, STEP + 8, WIDE), F32)] * 2,
        cost_estimate=pl.CostEstimate(flops=3 * 10**7, bytes_accessed=9 * 2**20, transcendentals=0),
        name="final_grads",
    )(streams, early, taps, masks, mix_grad, filtered, prod_grad, *nexts)


def step_along(value, axis, by):
    peers = lax.axis_size(axis)
    return lax.ppermute(value, axis, [(i, i + by) for i in range(peers) if 0 <= i + by < peers])


class Here:
    def __init__(self):
        self.x, self.w, self.z, self.y, self.c = [lax.axis_index(name) for name in DP + CTX]
        self.ctx = self.z * 8 + self.y * 2 + self.c
        self.dp = self.x * 2 + self.w

    def at_ctx(self, i):
        return (self.x, self.w, i // 8, lax.rem(i // 2, 4), lax.rem(i, 2))

    def at_dp(self, i):
        return (i // 2, lax.rem(i, 2), self.z, self.y, self.c)

    def along_x(self, by):
        return (lax.rem(self.x + by, 4), self.w, self.z, self.y, self.c)

    def along_y(self, by):
        return (self.x, self.w, self.z, lax.rem(self.y + by, 4), self.c)

    def along_z(self, by):
        return (self.x, self.w, lax.rem(self.z + by, 4), self.y, self.c)

    def across_w(self):
        return (self.x, 1 - self.w, self.z, self.y, self.c)

    def across_c(self):
        return (self.x, self.w, self.z, self.y, 1 - self.c)

    def before(self):
        return self.at_ctx(lax.rem(self.ctx + 31, 32))

    def meet(self):
        barrier = pltpu.get_barrier_semaphore()

        @pl.loop(1, 32)
        def _(p):
            place = self.at_ctx(lax.rem(self.ctx + p, 32))
            pl.semaphore_signal(barrier, inc=1, device_id=place, device_id_type=MESH)

        @pl.loop(1, 8)
        def _(p):
            place = self.at_dp(lax.rem(self.dp + p, 8))
            pl.semaphore_signal(barrier, inc=1, device_id=place, device_id_type=MESH)

        pl.semaphore_wait(barrier, 38)


class Links:
    def __init__(self, send, recv, local):
        self.send, self.recv, self.local = send, recv, local

    def to(self, n, place, src, dst):
        return pltpu.make_async_remote_copy(
            src_ref=src, dst_ref=dst, send_sem=self.send.at[n], recv_sem=self.recv.at[n],
            device_id=place, device_id_type=MESH,
        )

    def own(self, n, src, dst):
        return pltpu.make_async_copy(src, dst, self.local.at[n])

    def pairs(self, base, count, me, place, src, dst, same=False):
        def copy(p):
            peer = lax.rem(me + p, count)
            return self.to(base + p, place(peer), src if same else src.at[peer], dst.at[me])

        def start():
            @pl.loop(1, count)
            def _(p):
                copy(p).start()

        def finish():
            @pl.loop(1, count)
            def _(p):
                copy(p).wait()

        return start, finish


def sems(count):
    return [pltpu.SemaphoreType.DMA((count,)), pltpu.SemaphoreType.DMA((count,)), pltpu.SemaphoreType.DMA((8,))]


def anywhere():
    return pl.BlockSpec(memory_space=pl.ANY)


def comm_call(kernel, name, number, count, out_shape, args, in_specs=None, out_specs=None, scratch=()):
    return pl.pallas_call(
        kernel,
        out_shape=out_shape,
        in_specs=in_specs or [anywhere()] * len(args),
        out_specs=out_specs or [anywhere()] * len(out_shape),
        scratch_shapes=list(scratch) + sems(count),
        compiler_params=pltpu.CompilerParams(
            collective_id=number, has_side_effects=True, vmem_limit_bytes=40 * 1024 * 1024
        ),
        cost_estimate=pl.CostEstimate(flops=10**6, bytes_accessed=2**24, transcendentals=0),
        name=name,
    )(*args)


def b16(*shape):
    return jax.ShapeDtypeStruct(shape, BF16)


def gather_kernel(
    grad, weight, prod, filt, head,
    own_out, pair_out, prod_out, filt_out, top_out, head_out, send, recv, local,
):
    here = Here()
    links = Links(send, recv, local)
    x, w, y, c = here.x, here.w, here.y, here.c
    here.meet()
    right = links.to(0, here.along_x(1), grad, own_out.at[x])
    left = links.to(1, here.along_x(3), grad, own_out.at[x])
    share = links.to(2, here.across_w(), weight.at[c, y], pair_out.at[w, c, y])
    prods = links.pairs(16, 32, here.ctx, here.at_ctx, prod, prod_out)
    filts = links.pairs(48, 8, here.dp, here.at_dp, filt, filt_out, same=True)
    top = links.to(3, here.across_w(), grad.at[pl.ds(0, 64)], top_out)
    heads = links.to(4, here.before(), head, head_out)
    right.start()
    left.start()
    share.start()
    prods[0]()
    filts[0]()
    top.start()
    heads.start()
    locals_ = [
        links.own(0, grad, own_out.at[x]),
        links.own(1, weight, pair_out.at[w]),
        links.own(2, prod.at[here.ctx], prod_out.at[here.ctx]),
        links.own(3, filt, filt_out.at[here.dp]),
    ]
    for copy in locals_:
        copy.start()

    def piece(row, part=None):
        ref = pair_out.at[1 - w, c, row]
        return ref if part is None else ref.at[pl.ds(32 * part, 32)]

    def pass_on(n, place, row, part=None):
        copy = links.to(n, place, piece(row, part), piece(row, part))
        copy.start()
        return copy

    behind, ahead, far = lax.rem(y + 3, 4), lax.rem(y + 1, 4), lax.rem(y + 2, 4)
    share.wait_recv()
    up = pass_on(5, here.along_y(1), y)
    down = pass_on(6, here.along_y(3), y)
    over = [pass_on(7, here.across_c(), y)]
    up.wait_recv()
    up_half = pass_on(8, here.along_y(1), behind, 0)
    over.append(pass_on(9, here.across_c(), behind))
    down.wait_recv()
    down_half = pass_on(10, here.along_y(3), ahead, 1)
    over.append(pass_on(11, here.across_c(), ahead))

    x_behind, x_ahead = lax.rem(x + 3, 4), lax.rem(x + 1, 4)
    right.wait_recv()
    first = own_out.at[x_behind, pl.ds(0, 64)]
    right_half = links.to(12, here.along_x(1), first, first)
    right_half.start()
    left.wait_recv()
    second = own_out.at[x_ahead, pl.ds(64, 64)]
    left_half = links.to(13, here.along_x(3), second, second)
    left_half.start()
    up_half.wait_recv()
    down_half.wait_recv()
    over.append(pass_on(14, here.across_c(), far))
    prods[1]()
    filts[1]()
    for copy in over:
        copy.wait()
    for copy in (right_half, left_half, top, heads):
        copy.wait()
    for copy in (right, left, share, up, down, up_half, down_half):
        copy.wait_send()
    for copy in locals_:
        copy.wait()


def ring_steps(links, here, base, block, out):
    x = here.x
    half = block.shape[0] // 2
    right = links.to(base, here.along_x(1), block, out.at[x])
    left = links.to(base + 1, here.along_x(3), block, out.at[x])
    mine = links.own(7, block, out.at[x])
    first = out.at[lax.rem(x + 3, 4), pl.ds(0, half)]
    second = out.at[lax.rem(x + 1, 4), pl.ds(half, half)]
    right_half = links.to(base + 2, here.along_x(1), first, first)
    left_half = links.to(base + 3, here.along_x(3), second, second)

    def begin():
        right.start()
        left.start()
        mine.start()

    def forward():
        right.wait_recv()
        right_half.start()
        left.wait_recv()
        left_half.start()

    def finish():
        right_half.wait()
        left_half.wait()
        right.wait_send()
        left.wait_send()
        mine.wait()

    return begin, forward, finish


def middle_kernel(
    mix, filtered, grad, top, mix_out, filtered_out, bottom_out, ring_out, send, recv, local,
):
    here = Here()
    links = Links(send, recv, local)
    here.meet()
    mixes = links.pairs(0, 4, here.x, lambda i: (i, here.w, here.z, here.y, here.c), mix, mix_out)
    filts = links.pairs(16, 32, here.ctx, here.at_ctx, filtered, filtered_out)
    flip = links.to(4, here.across_w(), grad.at[pl.ds(64, 64)], bottom_out)
    ring = ring_steps(links, here, 5, top, ring_out)
    mixes[0]()
    filts[0]()
    ring[0]()
    flip.start()
    own = [
        links.own(0, mix.at[here.x], mix_out.at[here.x]),
        links.own(1, filtered.at[here.ctx], filtered_out.at[here.ctx]),
    ]
    for copy in own:
        copy.start()
    ring[1]()
    mixes[1]()
    filts[1]()
    flip.wait()
    ring[2]()
    for copy in own:
        copy.wait()


def spread_kernel(
    grad, mixed, bottom, mix_grad, filtered,
    grad_out, mixed_out, ring_out, mix_next_out, filtered_next_out, send, recv, local,
):
    here = Here()
    links = Links(send, recv, local)
    here.meet()
    grads = links.pairs(16, 32, here.ctx, here.at_ctx, grad, grad_out)
    mixes = links.pairs(48, 8, here.dp, here.at_dp, mixed, mixed_out)
    ring = ring_steps(links, here, 0, bottom, ring_out)
    nexts = [
        links.to(4, here.before(), mix_grad.at[:, pl.ds(0, 16)], mix_next_out),
        links.to(5, here.before(), filtered.at[:, pl.ds(0, 16)], filtered_next_out),
    ]
    grads[0]()
    mixes[0]()
    ring[0]()
    for copy in nexts:
        copy.start()
    own = [
        links.own(0, grad.at[here.ctx], grad_out.at[here.ctx]),
        links.own(1, mixed.at[here.dp], mixed_out.at[here.dp]),
    ]
    for copy in own:
        copy.start()
    ring[1]()
    mixes[1]()
    grads[1]()
    ring[2]()
    for copy in nexts + own:
        copy.wait()


def return_kernel(
    prod_grad, filt_grad, term,
    prod_out, filt_out, next_out, rows_out, half_ref, sum_ref, send, recv, local,
):
    here = Here()
    links = Links(send, recv, local)
    here.meet()
    half = links.to(0, here.across_c(), term.at[1 - here.c], half_ref)
    half.start()
    prods = links.pairs(16, 32, here.ctx, here.at_ctx, prod_grad, prod_out)
    filts = links.pairs(48, 8, here.dp, here.at_dp, filt_grad, filt_out)
    prods[0]()
    filts[0]()
    own = [
        links.own(0, prod_grad.at[here.ctx], prod_out.at[here.ctx]),
        links.own(1, filt_grad.at[here.dp], filt_out.at[here.dp]),
    ]
    for copy in own:
        copy.start()
    half.wait()

    @pl.loop(0, 16)
    def _(i):
        y, z = i // 4, lax.rem(i, 4)
        both = term[here.c, y, z].astype(F32) + half_ref[y, z].astype(F32)
        sum_ref[y, z] = both.astype(BF16)

    rows = links.pairs(8, 4, here.y, lambda i: (here.x, here.w, here.z, i, here.c), sum_ref, rows_out)
    rows[0]()
    mine = links.own(2, sum_ref.at[here.y], rows_out.at[here.y])
    mine.start()
    prods[1]()
    own[0].wait()
    ahead = links.to(1, here.before(), prod_out.at[:, pl.ds(0, 16)], next_out)
    ahead.start()
    filts[1]()
    rows[1]()
    ahead.wait()
    own[1].wait()
    mine.wait()


def last_kernel(
    parts_ref, rows_ref, total_ref, proj_ref,
    first, second, third, sum_ref, got_ref, send, recv, local,
):
    here = Here()
    links = Links(send, recv, local)
    here.meet()
    scatter = links.pairs(0, 32, here.ctx, here.at_ctx, parts_ref, first)
    share = links.pairs(32, 8, here.dp, here.at_dp, second.at[here.dp], second, same=True)
    gather = links.pairs(40, 32, here.ctx, here.at_ctx, third.at[here.ctx], third, same=True)
    zs = links.pairs(72, 4, here.z, lambda i: (here.x, here.w, i, here.y, here.c), sum_ref, got_ref)
    scatter[0]()
    first[here.ctx] = parts_ref[here.ctx]

    @pl.loop(0, 4)
    def _(z):
        total = rows_ref[0, z].astype(F32)
        for y in range(1, 4):
            total = total + rows_ref[y, z].astype(F32)
        sum_ref[z] = total.astype(BF16)

    zs[0]()
    got_ref[here.z] = sum_ref[here.z]
    scatter[1]()
    second[here.dp] = jnp.sum(first[...], axis=0)
    share[0]()
    share[1]()
    third[here.ctx] = jnp.sum(second[...], axis=0)
    gather[0]()
    zs[1]()
    total = got_ref[0].astype(F32)
    for z in range(1, 4):
        total = total + got_ref[z].astype(F32)
    proj_ref[...] = total * GRAD_SCALE
    gather[1]()
    total_ref[...] = third[...] * GRAD_SCALE


def weight_kernel(mixed_ref, own_ref, top_ref, bottom_ref, out_ref):
    rest = jnp.concatenate([top_ref[...], bottom_ref[...]], 0)
    total = dot32(mixed_ref[:, :512], own_ref[...]) + dot32(mixed_ref[:, 512:], rest)
    total = total.astype(BF16)
    for z in range(4):
        for y in range(4):
            for c in range(2):
                at = (z * 8 + y * 2 + c) * 16
                out_ref[c, y, z] = total[at : at + 16]


def weight_term_of(mixed, own, top, bottom):
    return pl.pallas_call(
        weight_kernel,
        grid=(8,),
        out_shape=jax.ShapeDtypeStruct((2, 4, 4, 16, 4096), BF16),
        in_specs=[pl.BlockSpec((512, 1024), lambda i: (0, 0)), flat_spec(512), flat_spec(256), flat_spec(256)],
        out_specs=pl.BlockSpec((2, 4, 4, 16, WIDE), lambda i: (0, 0, 0, 0, i)),
        compiler_params=pltpu.CompilerParams(vmem_limit_bytes=32 * 1024 * 1024),
        cost_estimate=pl.CostEstimate(flops=2**32, bytes_accessed=13 * 2**20, transcendentals=0),
        name="weight_term",
    )(mixed, own, top, bottom)


def body(streams, out_grad, proj_weight, long_filter, short_taps, doc_ids):
    rows = streams.shape[1]
    first_row = ((lax.axis_index(DP) * 32) + lax.axis_index(CTX)) * rows
    edge_ids = jnp.full((2,), -1, jnp.int32)
    id_rows = lax.dynamic_slice_in_dim(jnp.concatenate([edge_ids, doc_ids, edge_ids]), first_row, rows + 4)
    own_ids = id_rows[2 : 2 + rows]
    place = lax.axis_index(CTX) * rows + jnp.arange(rows)
    near = [
        jnp.logical_and(id_rows[2 + d : 2 + d + rows] == own_ids, jnp.logical_and(place + d >= 0, place + d < LENGTH))
        for d in (-1, -2, 1, 2)
    ]
    masks = jnp.stack(near + [jnp.zeros((rows,), bool)] * 4, axis=1).astype(F32)
    early = step_along(streams[:, rows - 2 :, :], CTX, 1)
    tables = tables_in()
    query, prod, head = short_filter(streams, early, short_taps, masks)
    own_groups, pair, prod_chan, filt, top, head_next = comm_call(
        gather_kernel, "gather", 1, 56,
        [b16(4, rows, 4096), b16(2, 2, 4, 64, 4096), b16(32, STEP, STEP), b16(8, 512, STEP), b16(64, 4096),
         jax.ShapeDtypeStruct((2, 8, 4096), F32)],
        (out_grad, proj_weight.reshape(2, 4, 64, 4096), prod, long_filter.astype(BF16), head),
    )
    own_groups = own_groups.reshape(512, 4096)
    mix_grad_groups = lax.dot_general(
        own_groups, pair.reshape(1024, 4096), (((1,), (1,)), ((), ())), preferred_element_type=F32
    ).astype(BF16)
    filtered_chan, spec_prod, spec_filt = filter_forward(prod_chan, filt.reshape(32, STEP, STEP), tables)
    mix_grad, filtered, bottom, top_ring = comm_call(
        middle_kernel, "middle", 2, 48,
        [b16(4, rows, 1024), b16(32, STEP, STEP), b16(64, 4096), b16(4, 64, 4096)],
        (mix_grad_groups.reshape(4, rows, 1024), filtered_chan, out_grad, top),
    )
    filtered_grad_chan, mixed, bottom_ring, mix_next, filtered_next = comm_call(
        spread_kernel, "spread", 3, 56,
        [b16(32, STEP, STEP), b16(8, rows, WIDE), b16(4, 64, 4096), b16(4, 16, 1024), b16(32, 16, STEP)],
        (filtered_grad_of(mix_grad, query), mixed_of(query, filtered), bottom, mix_grad, filtered),
    )
    w = lax.axis_index("w")
    mixed = mixed.reshape(4, 2, rows, WIDE)
    mixed = jnp.where(w == 0, mixed, mixed[:, ::-1])
    mixed_flip = mixed[:, 1].reshape(4, 2, 64, WIDE).transpose(1, 0, 2, 3).reshape(512, WIDE)
    mixed = jnp.concatenate([mixed[:, 0].reshape(512, WIDE), mixed_flip], 0).T
    weight_term = weight_term_of(mixed, own_groups, top_ring.reshape(256, 4096), bottom_ring.reshape(256, 4096))
    prod_grad_chan, filt_term = filter_backward(filtered_grad_chan, spec_prod, spec_filt, tables)
    prod_grad, filt_parts, prod_next, row_parts = comm_call(
        return_kernel, "returned", 4, 56,
        [b16(32, STEP, STEP), b16(8, 512, STEP), b16(32, 16, STEP), b16(4, 4, 16, 4096)],
        (prod_grad_chan, filt_term.reshape(8, 512, STEP), weight_term),
        in_specs=[anywhere(), anywhere(), vmem()],
        scratch=[pltpu.VMEM((4, 4, 16, 4096), BF16)] * 2,
    )
    stream_grads, tap_parts = final_grads(
        streams, early, short_taps, masks, mix_grad, filtered, prod_grad,
        (mix_next, filtered_next, prod_next, head_next),
    )
    filter_grad = jnp.sum(filt_parts.astype(F32), axis=0) * GRAD_SCALE
    taps, proj_grad = comm_call(
        last_kernel, "last", 5, 76,
        [jax.ShapeDtypeStruct((32, 16, STEP), F32), jax.ShapeDtypeStruct((16, 4096), F32)],
        (tap_parts, row_parts),
        in_specs=[vmem(), vmem()], out_specs=[vmem(), vmem()],
        scratch=[
            pltpu.VMEM((32, 16, STEP), F32), pltpu.VMEM((8, 16, STEP), F32), pltpu.VMEM((32, 16, STEP), F32),
            pltpu.VMEM((4, 16, 4096), BF16), pltpu.VMEM((4, 16, 4096), BF16),
        ],
    )
    tap_grad = taps[:, :9, :].transpose(1, 0, 2).reshape(3, 3, 4096)
    return stream_grads, proj_grad, filter_grad, tap_grad


def solution(mesh):
    devices = np.asarray(mesh.devices).reshape(4, 2, 4, 4, 2)
    fine = Mesh(devices, ("x", "w", "z", "y", "c"))
    every = DP + CTX
    return jax.shard_map(
        body,
        mesh=fine,
        in_specs=(P(None, every, None), P(every, None), P(DP, None), P(DP, CTX), P(), P()),
        out_specs=(P(None, every, None), P(every, None), P(DP, CTX), P()),
        check_vma=False,
    )
```

```python
import functools
import math

import jax
import jax.numpy as jnp
import numpy as np
from jax import lax
from jax.experimental import pallas as pl
from jax.experimental.pallas import tpu as pltpu
from jax.sharding import Mesh
from jax.sharding import PartitionSpec as P

DP = ("x", "w")
CTX = ("z", "y", "c")
F32 = jnp.float32
BF16 = jnp.bfloat16
LENGTH = 4096
TOTAL = 2 * LENGTH
SLOTS = 32
STEP = 128
WIDE = 512
GRAD_SCALE = float(32768) ** (-0.5)
MESH = pl.DeviceIdType.MESH


def split_table(table):
    return table.astype(BF16)


def make_tables():
    a = np.arange(32)
    b = np.arange(STEP)
    first = np.zeros((2 * SLOTS, 32))
    first[0] = 1.0
    first[1] = (-1.0) ** a
    for s in range(1, SLOTS):
        first[2 * s] = np.cos(2 * np.pi * a * s / 64)
        first[2 * s + 1] = -np.sin(2 * np.pi * a * s / 64)
    first_wide = np.kron(first, np.eye(8))
    last_wide = np.kron(first.T * (2.0 / TOTAL), np.eye(8))
    angle = 2 * np.pi * np.outer(b, b) / STEP
    cosine, sine = np.cos(angle), np.sin(angle)
    plain = np.block([[cosine, sine], [-sine, cosine]])
    special = np.zeros((2 * STEP, 2 * STEP))
    half = np.arange(64)
    even = 2 * np.pi * np.outer(half, b) / STEP
    odd = 2 * np.pi * np.outer(32 + 64 * half, b) / TOTAL
    special[:64, :STEP] = np.cos(even)
    special[64:128, STEP:] = np.cos(odd)
    special[128:192, :STEP] = -np.sin(even)
    special[128, :STEP] = (-1.0) ** b
    special[192:, STEP:] = -np.sin(odd)
    middle = np.stack([split_table(special), split_table(plain)])
    middle_back = np.stack([split_table(special.T), split_table(plain.T)])
    turn = 2 * np.pi * np.outer(np.arange(SLOTS), b) / TOTAL
    twist = np.concatenate([np.cos(turn), np.sin(turn)], 1).astype(np.float32)
    return split_table(first_wide), split_table(last_wide), middle, middle_back, twist


def dot32(a, b):
    return jnp.dot(a, b, preferred_element_type=F32)


def dot16(table, value):
    return dot32(table, value.astype(BF16))


def twisted(re, im, c, s):
    return re * c + im * s, im * c - re * s


def untwisted(re, im, c, s):
    return re * c - im * s, im * c + re * s


def halves_of(block):
    return [block[:, :8, :].reshape(256, STEP), block[:, 8:, :].reshape(256, STEP)]


def edge_rows(k):
    rows = lax.broadcasted_iota(jnp.int32, (STEP, STEP), 0)
    return jnp.logical_and(rows == 0, k == 0)


def filter_forward_kernel(
    prod_ref, filt_ref, first_ref, last_ref, mid_ref, back_ref, twist_ref,
    out_ref, spec_prod_ref, spec_filt_ref, yp_ref, yf_ref,
):
    first = first_ref[...]

    @pl.loop(0, 8, unroll=2)
    def _(h):
        rows = pl.ds(pl.multiple_of(16 * h, 16), 16)
        prods = halves_of(prod_ref[:, rows, :].astype(F32))
        filts = halves_of(filt_ref[:, :, rows, :].reshape(32, 16, STEP).astype(F32))
        for j in range(2):
            wide = dot32(first, jnp.concatenate([prods[j], filts[j]], 1).astype(BF16))
            at = pl.ds(pl.multiple_of(16 * h + 8 * j, 8), 8)
            yp_ref[:, at, :] = wide[:, :128].reshape(64, 8, STEP)
            yf_ref[:, at, :] = wide[:, 128:].reshape(64, 8, STEP)

    @pl.loop(0, SLOTS, unroll=4)
    def _(k):
        c, s = twist_ref[k, :STEP, :], twist_ref[k, STEP:, :]
        which = jnp.minimum(k, 1)
        pair = pl.ds(2 * k, 2)
        yp, yf = yp_ref[pair], yf_ref[pair]
        pr, pi = twisted(yp[0], yp[1], c, s)
        fr, fi = twisted(yf[0], yf[1], c, s)
        value = jnp.concatenate([jnp.concatenate([pr, pi], 0), jnp.concatenate([fr, fi], 0)], 1)
        spec = dot16(mid_ref[which], value)
        spec_prod_ref[k] = spec[:, :128]
        spec_filt_ref[k] = spec[:, 128:]
        pr, pi = spec[:128, :128], spec[128:, :128]
        fr, fi = spec[:128, 128:], spec[128:, 128:]
        edge = edge_rows(k)
        re = jnp.where(edge, 0.5 * (pr * fr), pr * fr - pi * fi)
        im = jnp.where(edge, 0.5 * (pi * fi), pr * fi + pi * fr)
        back = dot16(back_ref[which], jnp.concatenate([re, im], 0))
        re, im = untwisted(back[:128], back[128:], c, s)
        yp_ref[2 * k] = re
        yp_ref[2 * k + 1] = im

    last = last_ref[...]

    @pl.loop(0, 8, unroll=2)
    def _(h):
        halves = [yp_ref[:, pl.ds(pl.multiple_of(16 * h + 8 * j, 8), 8), :].reshape(512, STEP) for j in range(2)]
        out = dot16(last, jnp.concatenate(halves, 1))
        parts = [out[:, 128 * j : 128 * (j + 1)].reshape(32, 8, STEP) for j in range(2)]
        rows = pl.ds(pl.multiple_of(16 * h, 16), 16)
        out_ref[:, rows, :] = jnp.concatenate(parts, 1).astype(BF16)


def filter_backward_kernel(
    grad_ref, spec_prod_ref, spec_filt_ref, first_ref, last_ref, mid_ref, back_ref, twist_ref,
    prod_grad_ref, filt_grad_ref, yg_ref, yv_ref,
):
    first = first_ref[...]

    @pl.loop(0, 8, unroll=2)
    def _(h):
        rows = pl.ds(pl.multiple_of(16 * h, 16), 16)
        grads = halves_of(grad_ref[:, rows, :].astype(F32))
        grad = jnp.concatenate([grads[0], grads[1]], 1).astype(BF16)
        out = dot32(first, grad)
        for j in range(2):
            at = pl.ds(pl.multiple_of(16 * h + 8 * j, 8), 8)
            yg_ref[:, at, :] = out[:, 128 * j : 128 * (j + 1)].reshape(64, 8, STEP)

    @pl.loop(0, SLOTS, unroll=4)
    def _(k):
        c, s = twist_ref[k, :STEP, :], twist_ref[k, STEP:, :]
        which = jnp.minimum(k, 1)
        yg = yg_ref[pl.ds(2 * k, 2)]
        gr, gi = twisted(yg[0], yg[1], c, s)
        spec = dot16(mid_ref[which], jnp.concatenate([gr, gi], 0))
        gr, gi = spec[:128], spec[128:]
        edge = edge_rows(k)
        cols = []
        for ref in (spec_filt_ref, spec_prod_ref):
            hr, hi = ref[k, :STEP, :], ref[k, STEP:, :]
            re = jnp.where(edge, 0.5 * (hr * gr), hr * gr + hi * gi)
            im = jnp.where(edge, 0.5 * (hi * gi), hr * gi - hi * gr)
            cols.append(jnp.concatenate([re, im], 0))
        back = dot16(back_ref[which], jnp.concatenate(cols, 1))
        re, im = untwisted(back[:128, :128], back[128:, :128], c, s)
        yg_ref[2 * k] = re
        yg_ref[2 * k + 1] = im
        re, im = untwisted(back[:128, 128:], back[128:, 128:], c, s)
        yv_ref[2 * k] = re
        yv_ref[2 * k + 1] = im

    last = last_ref[...]

    @pl.loop(0, 8, unroll=2)
    def _(h):
        parts, other = [], []
        for j in range(2):
            at = pl.ds(pl.multiple_of(16 * h + 8 * j, 8), 8)
            value = jnp.concatenate([yg_ref[:, at, :].reshape(512, STEP), yv_ref[:, at, :].reshape(512, STEP)], 1)
            out = dot16(last, value)
            parts.append(out[:, :128].reshape(32, 8, STEP))
            other.append(out[:, 128:].reshape(32, 8, STEP))
        rows = pl.ds(pl.multiple_of(16 * h, 16), 16)
        prod_grad_ref[:, rows, :] = jnp.concatenate(parts, 1).astype(BF16)
        filt_grad_ref[:, rows, :] = jnp.concatenate(other, 1).astype(BF16)


def vmem():
    return pl.BlockSpec(memory_space=pltpu.VMEM)


def tables_in():
    first, last, middle, back, twist = make_tables()
    wide = jnp.broadcast_to(jnp.asarray(twist)[:, :, None], (SLOTS, 2 * STEP, STEP))
    return [jnp.asarray(first), jnp.asarray(last), jnp.asarray(middle), jnp.asarray(back), wide]


def convolved(ext_ref, taps, masks, stream):
    total = taps(0, stream) * ext_ref[stream, pl.ds(8, STEP), :]
    for i in (1, 2):
        total = total + taps(i, stream) * ext_ref[stream, pl.ds(8 - i, STEP), :] * masks[i - 1]
    return total


def fill_extended(rows, early, ext_ref):
    for s in range(3):
        ext_ref[s, pl.ds(6, 2), :] = early(s).astype(F32)[14:]
        ext_ref[s, pl.ds(8, STEP), :] = rows(s).astype(F32)


def rows_spec(lead, rows):
    return pl.BlockSpec((lead, rows, WIDE), lambda i: (0, 0, i))


def flat_spec(rows):
    return pl.BlockSpec((rows, WIDE), lambda i: (0, i))


def chan_spec(rows=STEP):
    return pl.BlockSpec((4, rows, STEP), lambda i: (i, 0, 0))


def slab_spec(rows=STEP):
    return pl.BlockSpec((1, rows, WIDE), lambda i: (i, 0, 0))


def pair_spec(rows=STEP):
    return pl.BlockSpec((1, rows, WIDE), lambda i: (i // 2, 0, i % 2))


def mask_spec():
    return pl.BlockSpec((STEP, 8), lambda i: (0, 0))


def lanes_of(ref):
    return jnp.concatenate([ref[j] for j in range(4)], 1)


def final_kernel(
    streams_ref, early_ref, taps_ref, masks_ref, mix_grad_ref, filtered_ref, prod_grad_ref,
    mix_next_ref, filtered_next_ref, prod_next_ref, head_next_ref,
    grads_ref, tap_ref, ext_ref, conv_ref,
):
    fill_extended(lambda s: streams_ref[s], lambda s: early_ref[s], ext_ref)
    taps = lambda i, s: taps_ref[i, s : s + 1, :]
    behind = [masks_ref[:, i : i + 1] for i in range(2)]
    ahead = [masks_ref[:, 2 + i : 3 + i] for i in range(2)]
    key = convolved(ext_ref, taps, behind, 1)
    value = convolved(ext_ref, taps, behind, 2)
    prod_grad = lanes_of(prod_grad_ref).astype(F32)
    prod_next = lanes_of(prod_next_ref).astype(F32)[:2]
    body = pl.ds(0, STEP)
    tail = pl.ds(STEP, 2)
    query_grad = mix_grad_ref[0].astype(F32) * lanes_of(filtered_ref).astype(F32)
    conv_ref[0, body, :] = query_grad.astype(BF16).astype(F32)
    query_next = mix_next_ref[0].astype(F32) * lanes_of(filtered_next_ref).astype(F32)
    conv_ref[0, tail, :] = query_next.astype(BF16).astype(F32)[:2]
    conv_ref[1, body, :] = prod_grad * value
    conv_ref[1, tail, :] = prod_next * head_next_ref[1, :2, :]
    conv_ref[2, body, :] = prod_grad * key
    conv_ref[2, tail, :] = prod_next * head_next_ref[0, :2, :]
    for s in range(3):
        here = conv_ref[s, body, :]
        grad = taps_ref[0, s : s + 1, :] * here
        sums = [jnp.sum(here * ext_ref[s, pl.ds(8, STEP), :], axis=0, keepdims=True)]
        for i in (1, 2):
            grad = grad + taps_ref[i, s : s + 1, :] * conv_ref[s, pl.ds(i, STEP), :] * ahead[i - 1]
            behind_rows = ext_ref[s, pl.ds(8 - i, STEP), :] * behind[i - 1]
            sums.append(jnp.sum(here * behind_rows, axis=0, keepdims=True))
        grads_ref[s] = grad.astype(BF16)
        for i in range(3):
            for j in range(4):
                tap_ref[j, 3 * i + s : 3 * i + s + 1, :] = sums[i][:, 128 * j : 128 * (j + 1)]
    for j in range(4):
        tap_ref[j, 9:16, :] = jnp.zeros((7, STEP), F32)


def final_grads(streams, early, taps, masks, mix_grad, filtered, prod_grad, nexts):
    return pl.pallas_call(
        final_kernel,
        grid=(8,),
        out_shape=[
            jax.ShapeDtypeStruct((3, STEP, 4096), BF16),
            jax.ShapeDtypeStruct((32, 16, STEP), F32),
        ],
        in_specs=[
            rows_spec(3, STEP), rows_spec(3, 16), rows_spec(3, 3), mask_spec(),
            pair_spec(), chan_spec(), chan_spec(), pair_spec(16), chan_spec(16), chan_spec(16), rows_spec(2, 8),
        ],
        out_specs=[rows_spec(3, STEP), chan_spec(16)],
        scratch_shapes=[pltpu.VMEM((3, STEP + 8, WIDE), F32)] * 2,
        cost_estimate=pl.CostEstimate(flops=3 * 10**7, bytes_accessed=9 * 2**20, transcendentals=0),
        name="final_grads",
    )(streams, early, taps, masks, mix_grad, filtered, prod_grad, *nexts)


class Here:
    def __init__(self):
        self.x, self.w, self.z, self.y, self.c = [lax.axis_index(name) for name in DP + CTX]
        self.ctx = self.z * 8 + self.y * 2 + self.c
        self.dp = self.x * 2 + self.w

    def at_ctx(self, i):
        return (self.x, self.w, i // 8, lax.rem(i // 2, 4), lax.rem(i, 2))

    def at_dp(self, i):
        return (i // 2, lax.rem(i, 2), self.z, self.y, self.c)

    def along_x(self, by):
        return (lax.rem(self.x + by, 4), self.w, self.z, self.y, self.c)

    def along_y(self, by):
        return (self.x, self.w, self.z, lax.rem(self.y + by, 4), self.c)

    def along_z(self, by):
        return (self.x, self.w, lax.rem(self.z + by, 4), self.y, self.c)

    def across_w(self):
        return (self.x, 1 - self.w, self.z, self.y, self.c)

    def across_c(self):
        return (self.x, self.w, self.z, self.y, 1 - self.c)

    def after(self):
        return self.at_ctx(lax.rem(self.ctx + 1, 32))

    def before(self):
        return self.at_ctx(lax.rem(self.ctx + 31, 32))

    def meet(self):
        barrier = pltpu.get_barrier_semaphore()

        @pl.loop(1, 32)
        def _(p):
            place = self.at_ctx(lax.rem(self.ctx + p, 32))
            pl.semaphore_signal(barrier, inc=1, device_id=place, device_id_type=MESH)

        @pl.loop(1, 8)
        def _(p):
            place = self.at_dp(lax.rem(self.dp + p, 8))
            pl.semaphore_signal(barrier, inc=1, device_id=place, device_id_type=MESH)

        pl.semaphore_wait(barrier, 38)


class Links:
    def __init__(self, send, recv, local):
        self.send, self.recv, self.local = send, recv, local

    def to(self, n, place, src, dst):
        return pltpu.make_async_remote_copy(
            src_ref=src, dst_ref=dst, send_sem=self.send.at[n], recv_sem=self.recv.at[n],
            device_id=place, device_id_type=MESH,
        )

    def own(self, n, src, dst):
        return pltpu.make_async_copy(src, dst, self.local.at[n])

    def pairs(self, base, count, me, place, src, dst, same=False, slot=None, source=None):
        def copy(p):
            peer = lax.rem(me + p, count)
            at = dst.at[slot(peer)] if slot else dst.at[me]
            block = source(peer) if source else src if same else src.at[peer]
            return self.to(base + p, place(peer), block, at)

        def start():
            @pl.loop(1, count)
            def _(p):
                copy(p).start()

        def finish():
            @pl.loop(1, count)
            def _(p):
                copy(p).wait()

        return start, finish


def sems(count):
    return [pltpu.SemaphoreType.DMA((count,)), pltpu.SemaphoreType.DMA((count,)), pltpu.SemaphoreType.DMA((16,))]


def anywhere():
    return pl.BlockSpec(memory_space=pl.ANY)


def comm_call(kernel, name, number, count, out_shape, args, in_specs=None, out_specs=None, scratch=(), room=40):
    return pl.pallas_call(
        kernel,
        out_shape=out_shape,
        in_specs=in_specs or [anywhere()] * len(args),
        out_specs=out_specs or [anywhere()] * len(out_shape),
        scratch_shapes=list(scratch) + sems(count),
        compiler_params=pltpu.CompilerParams(
            collective_id=number, has_side_effects=True, vmem_limit_bytes=room * 1024 * 1024
        ),
        cost_estimate=pl.CostEstimate(flops=10**6, bytes_accessed=2**24, transcendentals=0),
        name=name,
    )(*args)


def b16(*shape):
    return jax.ShapeDtypeStruct(shape, BF16)


def ring_steps(links, here, base, block, out):
    x = here.x
    half = block.shape[0] // 2
    right = links.to(base, here.along_x(1), block, out.at[x])
    left = links.to(base + 1, here.along_x(3), block, out.at[x])
    mine = links.own(7, block, out.at[x])
    first = out.at[lax.rem(x + 3, 4), pl.ds(0, half)]
    second = out.at[lax.rem(x + 1, 4), pl.ds(half, half)]
    right_half = links.to(base + 2, here.along_x(1), first, first)
    left_half = links.to(base + 3, here.along_x(3), second, second)

    def begin():
        right.start()
        left.start()
        mine.start()

    def forward():
        right.wait_recv()
        right_half.start()
        left.wait_recv()
        left_half.start()

    def finish():
        right_half.wait()
        left_half.wait()
        right.wait_send()
        left.wait_send()
        mine.wait()

    return begin, forward, finish


def mix_grad_product(own_ref, pair_ref, out_ref, slab, core):
    def step(k, total):
        cols = pl.ds(pl.multiple_of(k * 1024, 1024), 1024)
        left = own_ref[:, :, cols].reshape(512, 1024)
        right = pair_ref[slab, core, :, :, cols].reshape(256, 1024)
        return total + lax.dot_general(left, right, (((1,), (1,)), ((), ())), preferred_element_type=F32)

    total = lax.fori_loop(0, 4, step, jnp.zeros((512, 256), F32))
    cols = pl.ds(pl.multiple_of(slab * 512 + core * 256, 256), 256)
    out_ref[:, :, cols] = total.astype(BF16).reshape(4, STEP, 256)


def wide_cols(i):
    return pl.ds(pl.multiple_of(i * WIDE, WIDE), WIDE)


def first_kernel(
    grad, weight, filt, streams, taps_ref, masks_ref, first_ref, last_ref, mid_ref, back_ref, twist_ref,
    mix_out, filtered_out, early_ref, filter_out,
    head_out, mix_next_out, filtered_next_out, prod_out, prod_next_out, rows_out,
    own_out, spec_prod, spec_filt, flip_out, grads_out, mixed_out, turned_ref,
    pair_ref, prod_ref, filt_ref, yp_ref, yf_ref, mix_ref, filtered_ref, grads_ref, mixed_ref, flip_ref,
    query, head_ref, stage_ref, ext_ref,
    send, recv, local,
):
    here = Here()
    links = Links(send, recv, local)
    x, w, y, c = here.x, here.w, here.y, here.c
    here.meet()
    right = links.to(0, here.along_x(1), grad, own_out.at[x])
    left = links.to(1, here.along_x(3), grad, own_out.at[x])
    share = links.to(2, here.across_w(), weight.at[c, y], pair_ref.at[w, c, y])
    prods = links.pairs(16, 32, here.ctx, here.at_ctx, filtered_ref, prod_ref)
    early = links.to(137, here.after(), streams.at[:, pl.ds(112, 16)], early_ref)
    filts = links.pairs(48, 8, here.dp, here.at_dp, filt, filt_ref, same=True)
    flip = links.to(3, here.across_w(), grad, flip_ref)
    heads = links.to(4, here.before(), head_ref, head_out)
    share.start()
    early.start()
    right.start()
    left.start()
    locals_ = [
        links.own(0, grad, own_out.at[x]),
        links.own(1, weight, pair_ref.at[w]),
        links.own(3, filt, filt_ref.at[here.dp]),
    ]
    for copy in locals_:
        copy.start()
    filts[0]()
    masks = [masks_ref[:, i : i + 1] for i in range(2)]

    def fetch(i):
        slot = lax.rem(i, 2)
        return links.own(8 + slot, streams.at[:, :, wide_cols(i)], stage_ref.at[slot])

    fetch(0).start()
    early.wait_recv()

    @pl.loop(0, 8)
    def _(i):
        @pl.when(i < 7)
        def _():
            fetch(i + 1).start()

        fetch(i).wait()
        slot, cols = lax.rem(i, 2), wide_cols(i)
        fill_extended(lambda s: stage_ref[slot, s], lambda s: early_ref[s, :, cols], ext_ref)
        taps = lambda t, s: taps_ref[t, s : s + 1, cols]
        query[:, cols] = convolved(ext_ref, taps, masks, 0).astype(BF16)
        key = convolved(ext_ref, taps, masks, 1)
        value = convolved(ext_ref, taps, masks, 2)
        head_ref[0, :, cols] = key[:8]
        head_ref[1, :, cols] = value[:8]
        product = (key * value).astype(BF16)
        for j in range(4):
            filtered_ref[4 * i + j] = product[:, 128 * j : 128 * (j + 1)]

    def piece(row, part=None):
        ref = pair_ref.at[1 - w, c, row]
        return ref if part is None else ref.at[pl.ds(32 * part, 32)]

    def pass_on(n, place, row, part=None):
        copy = links.to(n, place, piece(row, part), piece(row, part))
        copy.start()
        return copy

    behind, ahead, far = lax.rem(y + 3, 4), lax.rem(y + 1, 4), lax.rem(y + 2, 4)
    share.wait_recv()
    up = pass_on(5, here.along_y(1), y)
    down = pass_on(6, here.along_y(3), y)
    over = [pass_on(7, here.across_c(), y)]
    prods[0]()
    prod_ref[here.ctx] = filtered_ref[here.ctx]
    heads.start()
    up.wait_recv()
    up_half = pass_on(8, here.along_y(1), behind, 0)
    over.append(pass_on(9, here.across_c(), behind))
    down.wait_recv()
    down_half = pass_on(10, here.along_y(3), ahead, 1)
    over.append(pass_on(11, here.across_c(), ahead))
    right.wait_recv()
    half = own_out.at[lax.rem(x + 3, 4), pl.ds(0, 64)]
    right_half = links.to(12, here.along_x(1), half, half)
    right_half.start()
    left.wait_recv()
    half = own_out.at[lax.rem(x + 1, 4), pl.ds(64, 64)]
    left_half = links.to(13, here.along_x(3), half, half)
    left_half.start()
    up_half.wait_recv()
    down_half.wait_recv()
    over.append(pass_on(14, here.across_c(), far))
    prods[1]()
    filts[1]()
    flip.start()
    for copy in locals_:
        copy.wait()

    filter_forward_kernel(
        prod_ref, filt_ref, first_ref, last_ref, mid_ref, back_ref, twist_ref,
        filtered_ref, spec_prod, spec_filt, yp_ref, yf_ref,
    )
    filtereds = links.pairs(56, 32, here.ctx, here.at_ctx, filtered_ref, filtered_out)
    filtereds[0]()
    filtered_out[here.ctx] = filtered_ref[here.ctx]

    right_half.wait()
    left_half.wait()
    for copy in over:
        copy.wait()

    @pl.loop(0, 4)
    def _(i):
        mix_grad_product(own_out, pair_ref, mix_ref, i // 2, lax.rem(i, 2))

    for copy in (right, left, share, up, down, up_half, down_half, early):
        copy.wait_send()
    mixes = links.pairs(88, 4, x, lambda i: (i, w, here.z, y, c), mix_ref, mix_out)
    mixes[0]()
    mix_out[x] = mix_ref[x]
    flip.wait()
    ring = ring_steps(links, here, 92, flip_ref, flip_out)
    mixes[1]()
    ring[0]()

    @pl.loop(0, 8)
    def _(i):
        mix = mix_out[i // 2, :, wide_cols(lax.rem(i, 2))]
        out = (mix.astype(F32) * query[:, wide_cols(i)].astype(F32)).astype(BF16)
        for j in range(4):
            grads_ref[4 * i + j] = out[:, 128 * j : 128 * (j + 1)]

    grads = links.pairs(96, 32, here.ctx, here.at_ctx, grads_ref, grads_out)
    grads[0]()
    grads_out[here.ctx] = grads_ref[here.ctx]
    mix_next = links.to(15, here.before(), mix_out.at[:, pl.ds(0, 16)], mix_next_out)
    mix_next.start()
    filtereds[1]()

    @pl.loop(0, 8)
    def _(i):
        filtered = jnp.concatenate([filtered_out[4 * i + j] for j in range(4)], 1)
        mixed_ref[i] = (query[:, wide_cols(i)].astype(F32) * filtered.astype(F32)).astype(BF16)

    mixeds = links.pairs(
        128, 8, here.dp, here.at_dp, mixed_ref, mixed_out,
        slot=lambda peer: lax.rem(w + lax.rem(peer, 2), 2) * 4 + x,
    )
    mixeds[0]()
    mixed_out[x] = mixed_ref[here.dp]
    filtered_next = links.to(136, here.before(), filtered_out.at[:, pl.ds(0, 16)], filtered_next_out)
    filtered_next.start()
    ring[1]()
    grads[1]()
    filter_backward_kernel(
        grads_out, spec_prod, spec_filt, first_ref, last_ref, mid_ref, back_ref, twist_ref,
        filtered_ref, grads_ref, yp_ref, yf_ref,
    )
    prod_grads = links.pairs(140, 32, here.ctx, here.at_ctx, filtered_ref, prod_out)
    prod_grads[0]()
    own_grad = links.own(4, filtered_ref.at[here.ctx], prod_out.at[here.ctx])
    own_grad.start()
    mixeds[1]()
    ring[2]()

    @pl.loop(0, 8)
    def _(i):
        at = pl.ds(pl.multiple_of(i * STEP, STEP), STEP)
        turned_ref[:, at] = mixed_out[i].astype(F32).T.astype(BF16)

    @pl.loop(0, 8)
    def _(i):
        cols = wide_cols(i)
        total = dot32(turned_ref[:, :512], own_out[:, :, cols].reshape(512, WIDE))
        total = total + dot32(turned_ref[:, 512:], flip_out[:, :, cols].reshape(512, WIDE))
        total = total.astype(BF16)
        for zz in range(4):
            for yy in range(4):
                for cc in range(2):
                    at = (zz * 8 + yy * 2 + cc) * 16
                    pair_ref[0, cc, yy, 16 * zz : 16 * (zz + 1), cols] = total[at : at + 16]

    half = links.to(138, here.across_c(), pair_ref.at[0, 1 - c], pair_ref.at[1, 0])
    half.start()
    filt_grads = links.pairs(
        172, 8, here.dp, here.at_dp, None, filt_ref, source=lambda peer: grads_ref.at[pl.ds(4 * peer, 4)]
    )
    filt_grads[0]()
    filt_ref[here.dp] = grads_ref[pl.ds(4 * here.dp, 4)]
    half.wait()

    @pl.loop(0, 16)
    def _(i):
        yy = i // 4
        at = pl.ds(pl.multiple_of(lax.rem(i, 4) * 16, 16), 16)
        both = pair_ref[0, c, yy, at, :].astype(F32) + pair_ref[1, 0, yy, at, :].astype(F32)
        pair_ref[1, 1, yy, at, :] = both.astype(BF16)

    rows = links.pairs(180, 4, y, lambda i: (x, w, here.z, i, c), pair_ref.at[1, 1], rows_out)
    rows[0]()
    mine = links.own(2, pair_ref.at[1, 1, y], rows_out.at[y])
    mine.start()
    prod_grads[1]()
    own_grad.wait()
    prod_next = links.to(139, here.before(), prod_out.at[:, pl.ds(0, 16)], prod_next_out)
    prod_next.start()
    filt_grads[1]()
    total = filt_ref[0].astype(F32)
    for i in range(1, 8):
        total = total + filt_ref[i].astype(F32)
    filter_out[...] = total * GRAD_SCALE
    rows[1]()
    for copy in (heads, mix_next, filtered_next, prod_next, mine):
        copy.wait()


def last_kernel(
    parts_ref, rows_ref, total_ref, proj_ref,
    first, second, third, sum_ref, got_ref, send, recv, local,
):
    here = Here()
    links = Links(send, recv, local)
    here.meet()
    scatter = links.pairs(0, 32, here.ctx, here.at_ctx, parts_ref, first)
    share = links.pairs(32, 8, here.dp, here.at_dp, second.at[here.dp], second, same=True)
    gather = links.pairs(40, 32, here.ctx, here.at_ctx, third.at[here.ctx], third, same=True)
    zs = links.pairs(72, 4, here.z, lambda i: (here.x, here.w, i, here.y, here.c), sum_ref, got_ref)
    scatter[0]()
    first[here.ctx] = parts_ref[here.ctx]

    @pl.loop(0, 4)
    def _(z):
        total = rows_ref[0, z].astype(F32)
        for y in range(1, 4):
            total = total + rows_ref[y, z].astype(F32)
        sum_ref[z] = total.astype(BF16)

    zs[0]()
    got_ref[here.z] = sum_ref[here.z]
    scatter[1]()
    second[here.dp] = jnp.sum(first[...], axis=0)
    share[0]()
    share[1]()
    third[here.ctx] = jnp.sum(second[...], axis=0)
    gather[0]()
    zs[1]()
    total = got_ref[0].astype(F32)
    for z in range(1, 4):
        total = total + got_ref[z].astype(F32)
    proj_ref[...] = total * GRAD_SCALE
    gather[1]()
    total_ref[...] = third[...] * GRAD_SCALE


def body(streams, out_grad, proj_weight, long_filter, short_taps, doc_ids):
    rows = streams.shape[1]
    first_row = ((lax.axis_index(DP) * 32) + lax.axis_index(CTX)) * rows
    edge_ids = jnp.full((2,), -1, jnp.int32)
    id_rows = lax.dynamic_slice_in_dim(jnp.concatenate([edge_ids, doc_ids, edge_ids]), first_row, rows + 4)
    own_ids = id_rows[2 : 2 + rows]
    place = lax.axis_index(CTX) * rows + jnp.arange(rows)
    near = [
        jnp.logical_and(id_rows[2 + d : 2 + d + rows] == own_ids, jnp.logical_and(place + d >= 0, place + d < LENGTH))
        for d in (-1, -2, 1, 2)
    ]
    masks = jnp.stack(near + [jnp.zeros((rows,), bool)] * 4, axis=1).astype(F32)
    tables = tables_in()
    blocks = b16(32, STEP, STEP)
    block_room = pltpu.VMEM((32, STEP, STEP), BF16)
    spec_room = pltpu.VMEM((SLOTS, 2 * STEP, STEP), F32)
    group_room = pltpu.VMEM((4, rows, 4096), BF16)
    slab_room = pltpu.VMEM((8, rows, WIDE), BF16)
    (mix_grad, filtered, early, filter_grad, head_next, mix_next, filtered_next, prod_grad, prod_next, row_parts) = comm_call(
        first_kernel, "first", 1, 184,
        [b16(4, rows, 1024), blocks, b16(3, 16, 4096), jax.ShapeDtypeStruct((4, STEP, STEP), F32),
         jax.ShapeDtypeStruct((2, 8, 4096), F32), b16(4, 16, 1024), b16(32, 16, STEP), blocks, b16(32, 16, STEP),
         b16(4, 64, 4096)],
        (out_grad, proj_weight.reshape(2, 4, 64, 4096), long_filter.astype(BF16).reshape(4, STEP, STEP), streams,
         short_taps, masks, *tables),
        in_specs=[anywhere()] * 4 + [vmem()] * 7,
        out_specs=[vmem()] * 4 + [anywhere()] * 6,
        scratch=[
            group_room, spec_room, spec_room, group_room, block_room, slab_room, pltpu.VMEM((WIDE, 1024), BF16),
            pltpu.VMEM((2, 2, 4, 64, 4096), BF16), block_room, pltpu.VMEM((8, 4, STEP, STEP), BF16),
            pltpu.VMEM((64, STEP, STEP), F32), pltpu.VMEM((64, STEP, STEP), F32),
            pltpu.VMEM((4, rows, 1024), BF16), block_room, block_room, slab_room, pltpu.VMEM((rows, 4096), BF16),
            pltpu.VMEM((rows, 4096), BF16), pltpu.VMEM((2, 8, 4096), F32),
            pltpu.VMEM((2, 3, rows, WIDE), BF16), pltpu.VMEM((3, rows + 8, WIDE), F32),
        ],
        room=58,
    )
    stream_grads, tap_parts = final_grads(
        streams, early, short_taps, masks, mix_grad, filtered, prod_grad,
        (mix_next, filtered_next, prod_next, head_next),
    )
    taps, proj_grad = comm_call(
        last_kernel, "last", 5, 76,
        [jax.ShapeDtypeStruct((32, 16, STEP), F32), jax.ShapeDtypeStruct((16, 4096), F32)],
        (tap_parts, row_parts.reshape(4, 4, 16, 4096)),
        in_specs=[vmem(), vmem()], out_specs=[vmem(), vmem()],
        scratch=[
            pltpu.VMEM((32, 16, STEP), F32), pltpu.VMEM((8, 16, STEP), F32), pltpu.VMEM((32, 16, STEP), F32),
            pltpu.VMEM((4, 16, 4096), BF16), pltpu.VMEM((4, 16, 4096), BF16),
        ],
    )
    tap_grad = taps[:, :9, :].transpose(1, 0, 2).reshape(3, 3, 4096)
    return stream_grads, proj_grad, filter_grad.reshape(512, STEP), tap_grad


def solution(mesh):
    devices = np.asarray(mesh.devices).reshape(4, 2, 4, 4, 2)
    fine = Mesh(devices, ("x", "w", "z", "y", "c"))
    every = DP + CTX
    return jax.shard_map(
        body,
        mesh=fine,
        in_specs=(P(None, every, None), P(every, None), P(DP, None), P(DP, CTX), P(), P()),
        out_specs=(P(None, every, None), P(every, None), P(DP, CTX), P()),
        check_vma=False,
    )
```

```python
import functools
import math

import jax
import jax.numpy as jnp
import numpy as np
from jax import lax
from jax.experimental import pallas as pl
from jax.experimental.pallas import tpu as pltpu
from jax.sharding import Mesh
from jax.sharding import PartitionSpec as P

DP = ("x", "w")
CTX = ("z", "y", "c")
F32 = jnp.float32
BF16 = jnp.bfloat16
LENGTH = 4096
TOTAL = 2 * LENGTH
SLOTS = 32
STEP = 128
WIDE = 512
GRAD_SCALE = float(32768) ** (-0.5)
MESH = pl.DeviceIdType.MESH


def split_table(table):
    return table.astype(BF16)


def make_tables():
    a = np.arange(32)
    b = np.arange(STEP)
    first = np.zeros((2 * SLOTS, 32))
    first[0] = 1.0
    first[1] = (-1.0) ** a
    for s in range(1, SLOTS):
        first[2 * s] = np.cos(2 * np.pi * a * s / 64)
        first[2 * s + 1] = -np.sin(2 * np.pi * a * s / 64)
    first_wide = np.kron(first, np.eye(8))
    last_wide = np.kron(first.T * (2.0 / TOTAL), np.eye(8))
    angle = 2 * np.pi * np.outer(b, b) / STEP
    cosine, sine = np.cos(angle), np.sin(angle)
    plain = np.block([[cosine, sine], [-sine, cosine]])
    special = np.zeros((2 * STEP, 2 * STEP))
    half = np.arange(64)
    even = 2 * np.pi * np.outer(half, b) / STEP
    odd = 2 * np.pi * np.outer(32 + 64 * half, b) / TOTAL
    special[:64, :STEP] = np.cos(even)
    special[64:128, STEP:] = np.cos(odd)
    special[128:192, :STEP] = -np.sin(even)
    special[128, :STEP] = (-1.0) ** b
    special[192:, STEP:] = -np.sin(odd)
    middle = np.stack([split_table(special), split_table(plain)])
    middle_back = np.stack([split_table(special.T), split_table(plain.T)])
    turn = 2 * np.pi * np.outer(np.arange(SLOTS), b) / TOTAL
    twist = np.concatenate([np.cos(turn), np.sin(turn)], 1).astype(np.float32)
    return split_table(first_wide), split_table(last_wide), middle, middle_back, twist


def dot32(a, b):
    return jnp.dot(a, b, preferred_element_type=F32)


def dot16(table, value):
    return dot32(table, value.astype(BF16))


def twisted(re, im, c, s):
    return re * c + im * s, im * c - re * s


def untwisted(re, im, c, s):
    return re * c - im * s, im * c + re * s


def halves_of(block):
    return [block[:, :8, :].reshape(256, STEP), block[:, 8:, :].reshape(256, STEP)]


def edge_rows(k):
    rows = lax.broadcasted_iota(jnp.int32, (STEP, STEP), 0)
    return jnp.logical_and(rows == 0, k == 0)


def filter_forward_kernel(
    prod_ref, filt_ref, first_ref, last_ref, mid_ref, back_ref, twist_ref,
    out_ref, spec_prod_ref, spec_filt_ref, yp_ref, yf_ref,
):
    first = first_ref[...]

    @pl.loop(0, 8, unroll=2)
    def _(h):
        rows = pl.ds(pl.multiple_of(16 * h, 16), 16)
        prods = halves_of(prod_ref[:, rows, :].astype(F32))
        slabs = [filt_ref[i % 2, i // 2, :, rows, :] for i in range(8)]
        filts = halves_of(jnp.concatenate(slabs, 0).astype(F32))
        for j in range(2):
            wide = dot32(first, jnp.concatenate([prods[j], filts[j]], 1).astype(BF16))
            at = pl.ds(pl.multiple_of(16 * h + 8 * j, 8), 8)
            yp_ref[:, at, :] = wide[:, :128].reshape(64, 8, STEP)
            yf_ref[:, at, :] = wide[:, 128:].reshape(64, 8, STEP)

    @pl.loop(0, SLOTS, unroll=4)
    def _(k):
        c, s = twist_ref[k, :STEP, :], twist_ref[k, STEP:, :]
        which = jnp.minimum(k, 1)
        pair = pl.ds(2 * k, 2)
        yp, yf = yp_ref[pair], yf_ref[pair]
        pr, pi = twisted(yp[0], yp[1], c, s)
        fr, fi = twisted(yf[0], yf[1], c, s)
        value = jnp.concatenate([jnp.concatenate([pr, pi], 0), jnp.concatenate([fr, fi], 0)], 1)
        spec = dot16(mid_ref[which], value)
        spec_prod_ref[k] = spec[:, :128]
        spec_filt_ref[k] = spec[:, 128:]
        pr, pi = spec[:128, :128], spec[128:, :128]
        fr, fi = spec[:128, 128:], spec[128:, 128:]
        edge = edge_rows(k)
        re = jnp.where(edge, 0.5 * (pr * fr), pr * fr - pi * fi)
        im = jnp.where(edge, 0.5 * (pi * fi), pr * fi + pi * fr)
        back = dot16(back_ref[which], jnp.concatenate([re, im], 0))
        re, im = untwisted(back[:128], back[128:], c, s)
        yp_ref[2 * k] = re
        yp_ref[2 * k + 1] = im

    last = last_ref[...]

    @pl.loop(0, 8, unroll=2)
    def _(h):
        halves = [yp_ref[:, pl.ds(pl.multiple_of(16 * h + 8 * j, 8), 8), :].reshape(512, STEP) for j in range(2)]
        out = dot16(last, jnp.concatenate(halves, 1))
        parts = [out[:, 128 * j : 128 * (j + 1)].reshape(32, 8, STEP) for j in range(2)]
        rows = pl.ds(pl.multiple_of(16 * h, 16), 16)
        out_ref[:, rows, :] = jnp.concatenate(parts, 1).astype(BF16)


def filter_backward_kernel(
    grad_ref, spec_prod_ref, spec_filt_ref, first_ref, last_ref, mid_ref, back_ref, twist_ref,
    prod_grad_ref, filt_grad_ref, yg_ref, yv_ref,
):
    first = first_ref[...]

    @pl.loop(0, 8, unroll=2)
    def _(h):
        rows = pl.ds(pl.multiple_of(16 * h, 16), 16)
        grads = halves_of(grad_ref[:, rows, :].astype(F32))
        grad = jnp.concatenate([grads[0], grads[1]], 1).astype(BF16)
        out = dot32(first, grad)
        for j in range(2):
            at = pl.ds(pl.multiple_of(16 * h + 8 * j, 8), 8)
            yg_ref[:, at, :] = out[:, 128 * j : 128 * (j + 1)].reshape(64, 8, STEP)

    @pl.loop(0, SLOTS, unroll=4)
    def _(k):
        c, s = twist_ref[k, :STEP, :], twist_ref[k, STEP:, :]
        which = jnp.minimum(k, 1)
        yg = yg_ref[pl.ds(2 * k, 2)]
        gr, gi = twisted(yg[0], yg[1], c, s)
        spec = dot16(mid_ref[which], jnp.concatenate([gr, gi], 0))
        gr, gi = spec[:128], spec[128:]
        edge = edge_rows(k)
        cols = []
        for ref in (spec_filt_ref, spec_prod_ref):
            hr, hi = ref[k, :STEP, :], ref[k, STEP:, :]
            re = jnp.where(edge, 0.5 * (hr * gr), hr * gr + hi * gi)
            im = jnp.where(edge, 0.5 * (hi * gi), hr * gi - hi * gr)
            cols.append(jnp.concatenate([re, im], 0))
        back = dot16(back_ref[which], jnp.concatenate(cols, 1))
        re, im = untwisted(back[:128, :128], back[128:, :128], c, s)
        yg_ref[2 * k] = re
        yg_ref[2 * k + 1] = im
        re, im = untwisted(back[:128, 128:], back[128:, 128:], c, s)
        yv_ref[2 * k] = re
        yv_ref[2 * k + 1] = im

    last = last_ref[...]

    @pl.loop(0, 8, unroll=2)
    def _(h):
        parts, other = [], []
        for j in range(2):
            at = pl.ds(pl.multiple_of(16 * h + 8 * j, 8), 8)
            value = jnp.concatenate([yg_ref[:, at, :].reshape(512, STEP), yv_ref[:, at, :].reshape(512, STEP)], 1)
            out = dot16(last, value)
            parts.append(out[:, :128].reshape(32, 8, STEP))
            other.append(out[:, 128:].reshape(32, 8, STEP))
        rows = pl.ds(pl.multiple_of(16 * h, 16), 16)
        prod_grad_ref[:, rows, :] = jnp.concatenate(parts, 1).astype(BF16)
        filt_grad_ref[:, rows, :] = jnp.concatenate(other, 1).astype(BF16)


def vmem():
    return pl.BlockSpec(memory_space=pltpu.VMEM)


def tables_in():
    first, last, middle, back, twist = make_tables()
    wide = jnp.asarray(np.ascontiguousarray(np.broadcast_to(twist[:, :, None], (SLOTS, 2 * STEP, STEP))))
    return [jnp.asarray(first), jnp.asarray(last), jnp.asarray(middle), jnp.asarray(back), wide]


def convolved(ext_ref, taps, masks, stream):
    total = taps(0, stream) * ext_ref[stream, pl.ds(8, STEP), :]
    for i in (1, 2):
        total = total + taps(i, stream) * ext_ref[stream, pl.ds(8 - i, STEP), :] * masks[i - 1]
    return total


def fill_extended(rows, early, ext_ref):
    for s in range(3):
        ext_ref[s, pl.ds(6, 2), :] = early(s).astype(F32)[14:]
        ext_ref[s, pl.ds(8, STEP), :] = rows(s).astype(F32)


class Here:
    def __init__(self):
        self.x, self.w, self.z, self.y, self.c = [lax.axis_index(name) for name in DP + CTX]
        self.ctx = self.z * 8 + self.y * 2 + self.c
        self.dp = self.x * 2 + self.w

    def at_ctx(self, i):
        return (self.x, self.w, i // 8, lax.rem(i // 2, 4), lax.rem(i, 2))

    def at_dp(self, i):
        return (i // 2, lax.rem(i, 2), self.z, self.y, self.c)

    def along_x(self, by):
        return (lax.rem(self.x + by, 4), self.w, self.z, self.y, self.c)

    def along_y(self, by):
        return (self.x, self.w, self.z, lax.rem(self.y + by, 4), self.c)

    def along_z(self, by):
        return (self.x, self.w, lax.rem(self.z + by, 4), self.y, self.c)

    def across_w(self):
        return (self.x, 1 - self.w, self.z, self.y, self.c)

    def across_c(self):
        return (self.x, self.w, self.z, self.y, 1 - self.c)

    def after(self):
        return self.at_ctx(lax.rem(self.ctx + 1, 32))

    def before(self):
        return self.at_ctx(lax.rem(self.ctx + 31, 32))

    def meet(self):
        barrier = pltpu.get_barrier_semaphore()

        @pl.loop(1, 32)
        def _(p):
            place = self.at_ctx(lax.rem(self.ctx + p, 32))
            pl.semaphore_signal(barrier, inc=1, device_id=place, device_id_type=MESH)

        @pl.loop(1, 8)
        def _(p):
            place = self.at_dp(lax.rem(self.dp + p, 8))
            pl.semaphore_signal(barrier, inc=1, device_id=place, device_id_type=MESH)

        pl.semaphore_wait(barrier, 38)


class Links:
    def __init__(self, send, recv, local):
        self.send, self.recv, self.local = send, recv, local

    def to(self, n, place, src, dst):
        return pltpu.make_async_remote_copy(
            src_ref=src, dst_ref=dst, send_sem=self.send.at[n], recv_sem=self.recv.at[n],
            device_id=place, device_id_type=MESH,
        )

    def apart(self, sent, got, place, src, dst):
        return pltpu.make_async_remote_copy(
            src_ref=src, dst_ref=dst, send_sem=self.send.at[sent], recv_sem=self.recv.at[got],
            device_id=place, device_id_type=MESH,
        )

    def own(self, n, src, dst):
        return pltpu.make_async_copy(src, dst, self.local.at[n])

    def pairs(self, base, count, me, place, src, dst, same=False, slot=None, source=None):
        def copy(p):
            peer = lax.rem(me + p, count)
            at = dst.at[slot(peer)] if slot else dst.at[me]
            block = source(peer) if source else src if same else src.at[peer]
            return self.to(base + p, place(peer), block, at)

        def start():
            @pl.loop(1, count)
            def _(p):
                copy(p).start()

        def finish():
            @pl.loop(1, count)
            def _(p):
                copy(p).wait()

        return start, finish


def sems(count):
    return [pltpu.SemaphoreType.DMA((count,)), pltpu.SemaphoreType.DMA((count,)), pltpu.SemaphoreType.DMA((16,))]


def anywhere():
    return pl.BlockSpec(memory_space=pl.ANY)


def comm_call(kernel, name, number, count, out_shape, args, in_specs=None, out_specs=None, scratch=(), room=40):
    return pl.pallas_call(
        kernel,
        out_shape=out_shape,
        in_specs=in_specs or [anywhere()] * len(args),
        out_specs=out_specs or [anywhere()] * len(out_shape),
        scratch_shapes=list(scratch) + sems(count),
        compiler_params=pltpu.CompilerParams(
            collective_id=number, has_side_effects=True, vmem_limit_bytes=room * 1024 * 1024
        ),
        cost_estimate=pl.CostEstimate(flops=10**6, bytes_accessed=2**24, transcendentals=0),
        name=name,
    )(*args)


def b16(*shape):
    return jax.ShapeDtypeStruct(shape, BF16)


def ring_steps(links, here, base, block, out, placed=False, local=7):
    x = here.x
    half = block.shape[0] // 2
    right = links.to(base, here.along_x(1), block, out.at[x])
    left = links.to(base + 1, here.along_x(3), block, out.at[x])
    mine = None if placed else links.own(local, block, out.at[x])
    first = out.at[lax.rem(x + 3, 4), pl.ds(0, half)]
    second = out.at[lax.rem(x + 1, 4), pl.ds(half, half)]
    right_half = links.to(base + 2, here.along_x(1), first, first)
    left_half = links.to(base + 3, here.along_x(3), second, second)

    def begin():
        right.start()
        left.start()
        if mine is not None:
            mine.start()

    def forward():
        right.wait_recv()
        right_half.start()
        left.wait_recv()
        left_half.start()

    def finish():
        right_half.wait()
        left_half.wait()
        right.wait_send()
        left.wait_send()
        if mine is not None:
            mine.wait()

    return begin, forward, finish


def mix_grad_product(own_ref, pair_ref, out_ref, slab, core):
    right = pair_ref[slab, core].reshape(256, 4096)
    cols = pl.ds(pl.multiple_of(slab * 512 + core * 256, 256), 256)
    for part in range(2):
        left = own_ref[2 * part : 2 * part + 2].reshape(256, 4096)
        total = lax.dot_general(left, right, (((1,), (1,)), ((), ())), preferred_element_type=F32)
        out_ref[2 * part : 2 * part + 2, :, cols] = total.astype(BF16).reshape(2, STEP, 256)


def wide_cols(i):
    return pl.ds(pl.multiple_of(i * WIDE, WIDE), WIDE)


def first_kernel(
    grad, weight, filt, streams, taps_ref, masks_ref, first_in, last_in, mid_in, back_in, twist_in,
    stream_out, proj_out, filter_out, tap_out,
    mix_out, filtered_out, early_ref, head_out, mix_next_out, filtered_next_out, prod_next_out, rows_ref, step_ref,
    result_ref, conv_ref, taps_part, tap_first, tap_second, tap_third, row_sum, row_got,
    filt_b, first_ref, last_ref, mid_ref, back_ref, twist_ref,
    own_out, spec_prod, spec_filt, flip_out, grads_out, mixed_out, turned_ref,
    pair_ref, prod_ref, filt_ref, yp_ref, yf_ref, mix_ref, filtered_ref, grads_ref,
    query, head_ref, stage_ref, ext_ref,
    send, recv, local,
):
    here = Here()
    links = Links(send, recv, local)
    x, w, y, c = here.x, here.w, here.y, here.c
    tables = [
        links.own(n, src, dst)
        for n, src, dst in (
            (4, first_in, first_ref), (5, mid_in, mid_ref), (6, twist_in, twist_ref), (12, back_in, back_ref),
            (13, last_in, last_ref),
        )
    ]
    for copy in tables:
        copy.start()
    filt_b[...] = filt[...].astype(BF16)
    here.meet()
    right = links.to(0, here.along_x(1), grad, own_out.at[x])
    left = links.to(1, here.along_x(3), grad, own_out.at[x])
    share = links.to(2, here.across_w(), weight.at[c, y], pair_ref.at[w, c, y])
    prods = links.pairs(16, 32, here.ctx, here.at_ctx, filtered_ref, prod_ref)
    early = links.to(137, here.after(), streams.at[:, pl.ds(112, 16)], early_ref)
    filt_share = links.to(48, here.across_w(), filt_b, filt_ref.at[w, x])
    filt_own = ring_steps(links, here, 184, filt_b, filt_ref.at[w], local=3)
    filt_other = ring_steps(links, here, 188, filt_ref.at[1 - w, x], filt_ref.at[1 - w], placed=True)
    flip = links.to(3, here.across_w(), grad, flip_out.at[x])
    heads = links.to(4, here.before(), head_ref, head_out)
    early.start()
    filt_share.start()
    filt_own[0]()
    share.start()
    right.start()
    left.start()
    locals_ = [
        links.own(0, grad, own_out.at[x]),
        links.own(1, weight, pair_ref.at[w]),
    ]
    for copy in locals_:
        copy.start()
    masks = [masks_ref[:, i : i + 1] for i in range(2)]

    def fetch(i):
        slot = lax.rem(i, 2)
        return links.own(8 + slot, streams.at[:, :, wide_cols(i)], stage_ref.at[slot])

    fetch(0).start()
    early.wait_recv()
    filt_share.wait()
    filt_other[0]()
    filt_own[1]()

    @pl.loop(0, 8)
    def _(i):
        @pl.when(i < 7)
        def _():
            fetch(i + 1).start()

        fetch(i).wait()
        slot, cols = lax.rem(i, 2), wide_cols(i)
        fill_extended(lambda s: stage_ref[slot, s], lambda s: early_ref[s, :, cols], ext_ref)
        taps = lambda t, s: taps_ref[t, s : s + 1, cols]
        query[:, cols] = convolved(ext_ref, taps, masks, 0).astype(BF16)
        key = convolved(ext_ref, taps, masks, 1)
        value = convolved(ext_ref, taps, masks, 2)
        head_ref[0, :, cols] = key[:8]
        head_ref[1, :, cols] = value[:8]
        product = (key * value).astype(BF16)
        for j in range(4):
            filtered_ref[4 * i + j] = product[:, 128 * j : 128 * (j + 1)]

    filt_other[1]()

    def piece(row, part=None):
        ref = pair_ref.at[1 - w, c, row]
        return ref if part is None else ref.at[pl.ds(32 * part, 32)]

    def pass_on(n, place, row, part=None):
        copy = links.to(n, place, piece(row, part), piece(row, part))
        copy.start()
        return copy

    behind, ahead, far = lax.rem(y + 3, 4), lax.rem(y + 1, 4), lax.rem(y + 2, 4)
    share.wait_recv()
    up = pass_on(5, here.along_y(1), y)
    down = pass_on(6, here.along_y(3), y)
    over = [pass_on(7, here.across_c(), y)]
    prods[0]()
    prod_ref[here.ctx] = filtered_ref[here.ctx]
    heads.start()
    up.wait_recv()
    up_half = pass_on(8, here.along_y(1), behind, 0)
    over.append(pass_on(9, here.across_c(), behind))
    down.wait_recv()
    down_half = pass_on(10, here.along_y(3), ahead, 1)
    over.append(pass_on(11, here.across_c(), ahead))
    right.wait_recv()
    half = own_out.at[lax.rem(x + 3, 4), pl.ds(0, 64)]
    right_half = links.to(12, here.along_x(1), half, half)
    right_half.start()
    left.wait_recv()
    half = own_out.at[lax.rem(x + 1, 4), pl.ds(64, 64)]
    left_half = links.to(13, here.along_x(3), half, half)
    left_half.start()
    flip.start()
    up_half.wait_recv()
    down_half.wait_recv()
    over.append(pass_on(14, here.across_c(), far))
    filt_own[2]()
    filt_other[2]()
    prods[1]()
    for copy in locals_:
        copy.wait()

    right_half.wait()
    left_half.wait()
    for copy in over:
        copy.wait()

    @pl.loop(0, 4)
    def _(i):
        mix_grad_product(own_out, pair_ref, mix_ref, i // 2, lax.rem(i, 2))

    for copy in (right, left, share, up, down, up_half, down_half, early):
        copy.wait_send()
    mixes = links.pairs(88, 4, x, lambda i: (i, w, here.z, y, c), mix_ref, mix_out)
    mixes[0]()
    mix_out[x] = mix_ref[x]
    for copy in tables:
        copy.wait()
    filter_forward_kernel(
        prod_ref, filt_ref, first_ref, last_ref, mid_ref, back_ref, twist_ref,
        filtered_ref, spec_prod, spec_filt, yp_ref, yf_ref,
    )
    filtereds = links.pairs(56, 32, here.ctx, here.at_ctx, filtered_ref, filtered_out)
    filtereds[0]()
    filtered_out[here.ctx] = filtered_ref[here.ctx]

    flip.wait()
    ring = ring_steps(links, here, 92, flip_out.at[x], flip_out, placed=True)
    mixes[1]()
    ring[0]()

    @pl.loop(0, 8)
    def _(i):
        mix = mix_out[i // 2, :, wide_cols(lax.rem(i, 2))]
        out = (mix.astype(F32) * query[:, wide_cols(i)].astype(F32)).astype(BF16)
        for j in range(4):
            grads_ref[4 * i + j] = out[:, 128 * j : 128 * (j + 1)]

    grads = links.pairs(96, 32, here.ctx, here.at_ctx, grads_ref, grads_out)
    grads[0]()
    grads_out[here.ctx] = grads_ref[here.ctx]
    mix_next = links.to(15, here.before(), mix_out.at[:, pl.ds(0, 16)], mix_next_out)
    mix_next.start()
    filtereds[1]()

    @pl.loop(0, 8)
    def _(i):
        filtered = jnp.concatenate([filtered_out[4 * i + j] for j in range(4)], 1)
        mixed = (query[:, wide_cols(i)].astype(F32) * filtered.astype(F32)).astype(BF16)
        mix_ref[i // 2, :, wide_cols(lax.rem(i, 2))] = mixed

    mixeds = links.pairs(
        128, 8, here.dp, here.at_dp, None, mixed_out,
        source=lambda peer: mix_ref.at[peer // 2, :, wide_cols(lax.rem(peer, 2))],
        slot=lambda peer: lax.rem(w + lax.rem(peer, 2), 2) * 4 + x,
    )
    mixeds[0]()
    mixed_out[x] = mix_ref[x, :, wide_cols(w)]
    filtered_next = links.to(136, here.before(), filtered_out.at[:, pl.ds(0, 16)], filtered_next_out)
    filtered_next.start()
    ring[1]()
    grads[1]()
    filter_backward_kernel(
        grads_out, spec_prod, spec_filt, first_ref, last_ref, mid_ref, back_ref, twist_ref,
        filtered_ref, grads_ref, yp_ref, yf_ref,
    )
    prod_grads = links.pairs(140, 32, here.ctx, here.at_ctx, filtered_ref, prod_ref)
    prod_grads[0]()
    prod_ref[here.ctx] = filtered_ref[here.ctx]
    mixeds[1]()
    ring[2]()

    @pl.loop(0, 8)
    def _(i):
        at = pl.ds(pl.multiple_of(i * STEP, STEP), STEP)
        turned_ref[:, at] = mixed_out[i].astype(F32).T.astype(BF16)

    @pl.loop(0, 8)
    def _(i):
        cols = wide_cols(i)
        total = dot32(turned_ref[:, :512], own_out[:, :, cols].reshape(512, WIDE))
        total = total + dot32(turned_ref[:, 512:], flip_out[:, :, cols].reshape(512, WIDE))
        total = total.astype(BF16)
        for zz in range(4):
            for yy in range(4):
                for cc in range(2):
                    at = (zz * 8 + yy * 2 + cc) * 16
                    pair_ref[0, cc, yy, 16 * zz : 16 * (zz + 1), cols] = total[at : at + 16]

    half = links.to(138, here.across_c(), pair_ref.at[0, 1 - c], pair_ref.at[1, 0])
    half.start()
    filt_grads = links.pairs(
        172, 8, here.dp, here.at_dp, None, filt_ref, slot=lambda peer: (w, x),
        source=lambda peer: grads_ref.at[pl.ds(4 * peer, 4)]
    )
    filt_grads[0]()
    filt_ref[w, x] = grads_ref[pl.ds(4 * here.dp, 4)]
    half.wait()

    @pl.loop(0, 16)
    def _(i):
        yy = i // 4
        at = pl.ds(pl.multiple_of(lax.rem(i, 4) * 16, 16), 16)
        both = pair_ref[0, c, yy, at, :].astype(F32) + pair_ref[1, 0, yy, at, :].astype(F32)
        pair_ref[1, 1, yy, at, :] = both.astype(BF16)

    up_place, down_place = here.along_y(1), here.along_y(3)
    y_up, y_down, y_far = lax.rem(y + 1, 4), lax.rem(y + 3, 4), lax.rem(y + 2, 4)
    far_steps = [
        links.to(180, up_place, pair_ref.at[1, 1, y_far, pl.ds(0, 32)], step_ref.at[0]),
        links.to(181, down_place, pair_ref.at[1, 1, y_far, pl.ds(32, 32)], step_ref.at[1]),
    ]
    for copy in far_steps:
        copy.start()
    for copy in far_steps:
        copy.wait()
    for side, row in ((0, y_up), (1, y_down)):
        for part in range(2):
            at = pl.ds(32 * side + 16 * part, 16)
            both = pair_ref[1, 1, row, at, :].astype(F32)
            both = both + step_ref[side, 16 * part : 16 * (part + 1), :].astype(F32)
            pair_ref[1, 1, row, at, :] = both.astype(BF16)
    near_steps = [
        links.to(182, up_place, pair_ref.at[1, 1, y_up], rows_ref.at[0]),
        links.to(183, down_place, pair_ref.at[1, 1, y_down], rows_ref.at[1]),
    ]
    for copy in near_steps:
        copy.start()
    prod_grads[1]()
    prod_next = links.to(139, here.before(), prod_ref.at[:, pl.ds(0, 16)], prod_next_out)
    prod_next.start()
    filt_grads[1]()
    total = filt_ref[0, 0].astype(F32)
    for i in range(1, 8):
        total = total + filt_ref[i % 2, i // 2].astype(F32)
    filter_out[...] = total * GRAD_SCALE
    for copy in (heads, mix_next, filtered_next, prod_next):
        copy.wait()
    ahead = [masks_ref[:, 2 + i : 3 + i] for i in range(2)]

    def store(i):
        slot = lax.rem(i, 2)
        return links.own(10 + slot, result_ref.at[slot], stream_out.at[:, :, wide_cols(i)])

    fetch(0).start()

    @pl.loop(0, 8)
    def _(i):
        @pl.when(i < 7)
        def _():
            fetch(i + 1).start()

        @pl.when(i >= 2)
        def _():
            store(i - 2).wait()

        fetch(i).wait()
        slot, cols = lax.rem(i, 2), wide_cols(i)
        mix_cols = wide_cols(lax.rem(i, 2))
        fill_extended(lambda s: stage_ref[slot, s], lambda s: early_ref[s, :, cols], ext_ref)
        taps = lambda t, s: taps_ref[t, s : s + 1, cols]
        key = convolved(ext_ref, taps, masks, 1)
        value = convolved(ext_ref, taps, masks, 2)

        def lanes(ref):
            return jnp.concatenate([ref[4 * i + j] for j in range(4)], 1).astype(F32)

        product_grad = lanes(prod_ref)
        product_next = lanes(prod_next_out)[:2]
        inner, outer = pl.ds(0, STEP), pl.ds(STEP, 2)
        query_grad = mix_out[i // 2, :, mix_cols].astype(F32) * lanes(filtered_out)
        conv_ref[0, inner, :] = query_grad.astype(BF16).astype(F32)
        query_next = mix_next_out[i // 2, :, mix_cols].astype(F32) * lanes(filtered_next_out)
        conv_ref[0, outer, :] = query_next.astype(BF16).astype(F32)[:2]
        conv_ref[1, inner, :] = product_grad * value
        conv_ref[1, outer, :] = product_next * head_out[1, :2, cols]
        conv_ref[2, inner, :] = product_grad * key
        conv_ref[2, outer, :] = product_next * head_out[0, :2, cols]
        for s in range(3):
            at_here = conv_ref[s, inner, :]
            grad_rows = taps(0, s) * at_here
            sums = [jnp.sum(at_here * ext_ref[s, pl.ds(8, STEP), :], axis=0, keepdims=True)]
            for t in (1, 2):
                grad_rows = grad_rows + taps(t, s) * conv_ref[s, pl.ds(t, STEP), :] * ahead[t - 1]
                behind_rows = ext_ref[s, pl.ds(8 - t, STEP), :] * masks[t - 1]
                sums.append(jnp.sum(at_here * behind_rows, axis=0, keepdims=True))
            result_ref[slot, s] = grad_rows.astype(BF16)
            for t in range(3):
                for j in range(4):
                    taps_part[4 * i + j, 3 * t + s : 3 * t + s + 1, :] = sums[t][:, 128 * j : 128 * (j + 1)]
        for j in range(4):
            taps_part[4 * i + j, 9:16, :] = jnp.zeros((7, STEP), F32)
        store(i).start()
        for j in range(4):
            peer = 4 * i + j

            @pl.when(peer != here.ctx)
            def _():
                links.apart(
                    192 + peer, 192 + here.ctx, here.at_ctx(peer), taps_part.at[peer], tap_first.at[here.ctx]
                ).start()

    spread = links.pairs(224, 8, here.dp, here.at_dp, tap_second.at[here.dp], tap_second, same=True)
    gather = links.pairs(232, 32, here.ctx, here.at_ctx, tap_third.at[here.ctx], tap_third, same=True)
    zs = links.pairs(264, 4, here.z, lambda i: (x, w, i, y, c), row_sum, row_got)
    tap_first[here.ctx] = taps_part[here.ctx]
    for copy in near_steps:
        copy.wait()

    @pl.loop(0, 4)
    def _(i):
        at = pl.ds(pl.multiple_of(i * 16, 16), 16)
        total = pair_ref[1, 1, y, at, :].astype(F32)
        for k in range(2):
            total = total + rows_ref[k, at, :].astype(F32)
        row_sum[i] = total.astype(BF16)

    zs[0]()
    row_got[here.z] = row_sum[here.z]

    @pl.loop(1, 32)
    def _(p):
        peer = lax.rem(here.ctx + p, 32)
        links.apart(192 + peer, 192 + peer, here.at_ctx(peer), taps_part.at[peer], tap_first.at[peer]).wait()

    tap_second[here.dp] = jnp.sum(tap_first[...], axis=0)
    spread[0]()
    spread[1]()
    tap_third[here.ctx] = jnp.sum(tap_second[...], axis=0)
    gather[0]()
    zs[1]()
    total = row_got[0].astype(F32)
    for i in range(1, 4):
        total = total + row_got[i].astype(F32)
    proj_out[...] = total * GRAD_SCALE
    store(6).wait()
    store(7).wait()
    gather[1]()
    totals = jnp.concatenate([tap_third[j] for j in range(32)], 1) * GRAD_SCALE
    for t in range(3):
        tap_out[t] = totals[3 * t : 3 * t + 3]


def body(streams, out_grad, proj_weight, long_filter, short_taps, doc_ids):
    rows = streams.shape[1]
    first_row = ((lax.axis_index(DP) * 32) + lax.axis_index(CTX)) * rows
    edge_ids = jnp.full((2,), -1, jnp.int32)
    id_rows = lax.dynamic_slice_in_dim(jnp.concatenate([edge_ids, doc_ids, edge_ids]), first_row, rows + 4)
    own_ids = id_rows[2 : 2 + rows]
    place = lax.axis_index(CTX) * rows + jnp.arange(rows)
    near = [
        jnp.logical_and(id_rows[2 + d : 2 + d + rows] == own_ids, jnp.logical_and(place + d >= 0, place + d < LENGTH))
        for d in (-1, -2, 1, 2)
    ]
    masks = jnp.stack(near + [jnp.zeros((rows,), bool)] * 4, axis=1).astype(F32)
    tables = tables_in()
    block_room = pltpu.VMEM((32, STEP, STEP), BF16)
    spec_room = pltpu.VMEM((SLOTS, 2 * STEP, STEP), F32)
    group_room = pltpu.VMEM((4, rows, 4096), BF16)
    slab_room = pltpu.VMEM((8, rows, WIDE), BF16)
    half_blocks = pltpu.VMEM((32, 16, STEP), BF16)
    part_room = pltpu.VMEM((32, 16, STEP), F32)
    head_room = pltpu.VMEM((2, 8, 4096), F32)
    stage_room = pltpu.VMEM((2, 3, rows, WIDE), BF16)
    ext_room = pltpu.VMEM((3, rows + 8, WIDE), F32)
    mix_room = pltpu.VMEM((4, rows, 1024), BF16)
    row_room = pltpu.VMEM((4, 16, 4096), BF16)
    stream_grads, proj_grad, filter_grad, taps = comm_call(
        first_kernel, "hyena_backward", 1, 268,
        [b16(3, rows, 4096), jax.ShapeDtypeStruct((16, 4096), F32), jax.ShapeDtypeStruct((4, STEP, STEP), F32),
         jax.ShapeDtypeStruct((3, 3, 4096), F32)],
        (out_grad, proj_weight.reshape(2, 4, 64, 4096), long_filter.reshape(4, STEP, STEP), streams,
         short_taps, masks, *tables),
        in_specs=[anywhere()] * 2 + [vmem(), anywhere(), vmem(), vmem()] + [anywhere()] * 5,
        out_specs=[anywhere()] + [vmem()] * 3,
        scratch=[
            mix_room, block_room, pltpu.VMEM((3, 16, 4096), BF16), head_room, pltpu.VMEM((4, 16, 1024), BF16),
            half_blocks, half_blocks, pltpu.VMEM((2, 64, 4096), BF16), pltpu.VMEM((2, 32, 4096), BF16),
            stage_room, ext_room,
            part_room, part_room, pltpu.VMEM((8, 16, STEP), F32), part_room, row_room, row_room,
            pltpu.VMEM((4, STEP, STEP), BF16), *[pltpu.VMEM(table.shape, table.dtype) for table in tables],
            group_room, spec_room, spec_room, group_room, block_room, slab_room, pltpu.VMEM((WIDE, 1024), BF16),
            pltpu.VMEM((2, 2, 4, 64, 4096), BF16), block_room, pltpu.VMEM((2, 4, 4, STEP, STEP), BF16),
            pltpu.VMEM((64, STEP, STEP), F32), pltpu.VMEM((64, STEP, STEP), F32),
            mix_room, block_room, block_room, pltpu.VMEM((rows, 4096), BF16), head_room, stage_room, ext_room,
        ],
        room=62,
    )
    return stream_grads, proj_grad, filter_grad.reshape(512, STEP), taps


def solution(mesh):
    devices = np.asarray(mesh.devices).reshape(4, 2, 4, 4, 2)
    fine = Mesh(devices, ("x", "w", "z", "y", "c"))
    every = DP + CTX
    return jax.shard_map(
        body,
        mesh=fine,
        in_specs=(P(None, every, None), P(every, None), P(DP, None), P(DP, CTX), P(), P()),
        out_specs=(P(None, every, None), P(every, None), P(DP, CTX), P()),
        check_vma=False,
    )
```

```python
import functools
import math

import jax
import jax.numpy as jnp
import numpy as np
from jax import lax
from jax.experimental import pallas as pl
from jax.experimental.pallas import tpu as pltpu
from jax.sharding import Mesh
from jax.sharding import PartitionSpec as P

DP = ("x", "w")
CTX = ("z", "y", "c")
F32 = jnp.float32
BF16 = jnp.bfloat16
LENGTH = 4096
TOTAL = 2 * LENGTH
SLOTS = 32
STEP = 128
WIDE = 512
GRAD_SCALE = float(32768) ** (-0.5)
MESH = pl.DeviceIdType.MESH


def split_table(table):
    return table.astype(BF16)


def make_tables():
    a = np.arange(32)
    b = np.arange(STEP)
    first = np.zeros((2 * SLOTS, 32))
    first[0] = 1.0
    first[1] = (-1.0) ** a
    for s in range(1, SLOTS):
        first[2 * s] = np.cos(2 * np.pi * a * s / 64)
        first[2 * s + 1] = -np.sin(2 * np.pi * a * s / 64)
    first_wide = np.kron(first, np.eye(8))
    last_wide = np.kron(first.T * (2.0 / TOTAL), np.eye(8))
    angle = 2 * np.pi * np.outer(b, b) / STEP
    cosine, sine = np.cos(angle), np.sin(angle)
    plain = np.block([[cosine, sine], [-sine, cosine]])
    special = np.zeros((2 * STEP, 2 * STEP))
    half = np.arange(64)
    even = 2 * np.pi * np.outer(half, b) / STEP
    odd = 2 * np.pi * np.outer(32 + 64 * half, b) / TOTAL
    special[:64, :STEP] = np.cos(even)
    special[64:128, STEP:] = np.cos(odd)
    special[128:192, :STEP] = -np.sin(even)
    special[128, :STEP] = (-1.0) ** b
    special[192:, STEP:] = -np.sin(odd)
    middle = np.stack([split_table(special), split_table(plain)])
    middle_back = np.stack([split_table(special.T), split_table(plain.T)])
    turn = 2 * np.pi * np.outer(np.arange(SLOTS), b) / TOTAL
    twist = np.concatenate([np.cos(turn), np.sin(turn)], 1).astype(np.float32)
    return split_table(first_wide), split_table(last_wide), middle, middle_back, twist


def dot32(a, b):
    return jnp.dot(a, b, preferred_element_type=F32)


def dot16(table, value):
    return dot32(table, value.astype(BF16))


def twisted(re, im, c, s):
    return re * c + im * s, im * c - re * s


def untwisted(re, im, c, s):
    return re * c - im * s, im * c + re * s


def halves_of(block):
    return [block[:, :8, :].reshape(256, STEP), block[:, 8:, :].reshape(256, STEP)]


def edge_rows(k):
    rows = lax.broadcasted_iota(jnp.int32, (STEP, STEP), 0)
    return jnp.logical_and(rows == 0, k == 0)


def filter_forward_kernel(
    prod_ref, filt_ref, first_ref, last_ref, mid_ref, back_ref, twist_ref,
    out_ref, spec_prod_ref, spec_filt_ref, yp_ref, yf_ref,
):
    first = first_ref[...]

    @pl.loop(0, 8, unroll=2)
    def _(h):
        rows = pl.ds(pl.multiple_of(16 * h, 16), 16)
        prods = halves_of(prod_ref[:, rows, :].astype(F32))
        slabs = [filt_ref[i % 2, i // 2, :, rows, :] for i in range(8)]
        filts = halves_of(jnp.concatenate(slabs, 0).astype(F32))
        for j in range(2):
            wide = dot32(first, jnp.concatenate([prods[j], filts[j]], 1).astype(BF16))
            at = pl.ds(pl.multiple_of(16 * h + 8 * j, 8), 8)
            yp_ref[:, at, :] = wide[:, :128].reshape(64, 8, STEP)
            yf_ref[:, at, :] = wide[:, 128:].reshape(64, 8, STEP)

    @pl.loop(0, SLOTS, unroll=4)
    def _(k):
        c, s = twist_ref[k, :STEP, :], twist_ref[k, STEP:, :]
        which = jnp.minimum(k, 1)
        pair = pl.ds(2 * k, 2)
        yp, yf = yp_ref[pair], yf_ref[pair]
        pr, pi = twisted(yp[0], yp[1], c, s)
        fr, fi = twisted(yf[0], yf[1], c, s)
        value = jnp.concatenate([jnp.concatenate([pr, pi], 0), jnp.concatenate([fr, fi], 0)], 1)
        spec = dot16(mid_ref[which], value)
        spec_prod_ref[k] = spec[:, :128]
        spec_filt_ref[k] = spec[:, 128:]
        pr, pi = spec[:128, :128], spec[128:, :128]
        fr, fi = spec[:128, 128:], spec[128:, 128:]
        edge = edge_rows(k)
        re = jnp.where(edge, 0.5 * (pr * fr), pr * fr - pi * fi)
        im = jnp.where(edge, 0.5 * (pi * fi), pr * fi + pi * fr)
        back = dot16(back_ref[which], jnp.concatenate([re, im], 0))
        re, im = untwisted(back[:128], back[128:], c, s)
        yp_ref[2 * k] = re
        yp_ref[2 * k + 1] = im

    last = last_ref[...]

    @pl.loop(0, 8, unroll=2)
    def _(h):
        halves = [yp_ref[:, pl.ds(pl.multiple_of(16 * h + 8 * j, 8), 8), :].reshape(512, STEP) for j in range(2)]
        out = dot16(last, jnp.concatenate(halves, 1))
        parts = [out[:, 128 * j : 128 * (j + 1)].reshape(32, 8, STEP) for j in range(2)]
        rows = pl.ds(pl.multiple_of(16 * h, 16), 16)
        out_ref[:, rows, :] = jnp.concatenate(parts, 1).astype(BF16)


def filter_backward_kernel(
    grad_ref, spec_prod_ref, spec_filt_ref, first_ref, last_ref, mid_ref, back_ref, twist_ref,
    prod_grad_ref, filt_grad_ref, yg_ref, yv_ref,
):
    first = first_ref[...]

    @pl.loop(0, 8, unroll=2)
    def _(h):
        rows = pl.ds(pl.multiple_of(16 * h, 16), 16)
        grads = halves_of(grad_ref[:, rows, :].astype(F32))
        grad = jnp.concatenate([grads[0], grads[1]], 1).astype(BF16)
        out = dot32(first, grad)
        for j in range(2):
            at = pl.ds(pl.multiple_of(16 * h + 8 * j, 8), 8)
            yg_ref[:, at, :] = out[:, 128 * j : 128 * (j + 1)].reshape(64, 8, STEP)

    @pl.loop(0, SLOTS, unroll=4)
    def _(k):
        c, s = twist_ref[k, :STEP, :], twist_ref[k, STEP:, :]
        which = jnp.minimum(k, 1)
        yg = yg_ref[pl.ds(2 * k, 2)]
        gr, gi = twisted(yg[0], yg[1], c, s)
        spec = dot16(mid_ref[which], jnp.concatenate([gr, gi], 0))
        gr, gi = spec[:128], spec[128:]
        edge = edge_rows(k)
        cols = []
        for ref in (spec_filt_ref, spec_prod_ref):
            hr, hi = ref[k, :STEP, :], ref[k, STEP:, :]
            re = jnp.where(edge, 0.5 * (hr * gr), hr * gr + hi * gi)
            im = jnp.where(edge, 0.5 * (hi * gi), hr * gi - hi * gr)
            cols.append(jnp.concatenate([re, im], 0))
        back = dot16(back_ref[which], jnp.concatenate(cols, 1))
        re, im = untwisted(back[:128, :128], back[128:, :128], c, s)
        yg_ref[2 * k] = re
        yg_ref[2 * k + 1] = im
        re, im = untwisted(back[:128, 128:], back[128:, 128:], c, s)
        yv_ref[2 * k] = re
        yv_ref[2 * k + 1] = im

    last = last_ref[...]

    @pl.loop(0, 8, unroll=2)
    def _(h):
        parts, other = [], []
        for j in range(2):
            at = pl.ds(pl.multiple_of(16 * h + 8 * j, 8), 8)
            value = jnp.concatenate([yg_ref[:, at, :].reshape(512, STEP), yv_ref[:, at, :].reshape(512, STEP)], 1)
            out = dot16(last, value)
            parts.append(out[:, :128].reshape(32, 8, STEP))
            other.append(out[:, 128:].reshape(32, 8, STEP))
        rows = pl.ds(pl.multiple_of(16 * h, 16), 16)
        prod_grad_ref[:, rows, :] = jnp.concatenate(parts, 1).astype(BF16)
        filt_grad_ref[:, rows, :] = jnp.concatenate(other, 1).astype(BF16)


def vmem():
    return pl.BlockSpec(memory_space=pltpu.VMEM)


def tables_in():
    first, last, middle, back, twist = make_tables()
    wide = jnp.asarray(np.ascontiguousarray(np.broadcast_to(twist[:, :, None], (SLOTS, 2 * STEP, STEP))))
    return [jnp.asarray(first), jnp.asarray(last), jnp.asarray(middle), jnp.asarray(back), wide]


def convolved(ext_ref, taps, masks, stream):
    total = taps(0, stream) * ext_ref[stream, pl.ds(8, STEP), :]
    for i in (1, 2):
        total = total + taps(i, stream) * ext_ref[stream, pl.ds(8 - i, STEP), :] * masks[i - 1]
    return total


def fill_extended(rows, early, ext_ref):
    for s in range(3):
        ext_ref[s, pl.ds(6, 2), :] = early(s).astype(F32)[14:]
        ext_ref[s, pl.ds(8, STEP), :] = rows(s).astype(F32)


class Here:
    def __init__(self):
        self.x, self.w, self.z, self.y, self.c = [lax.axis_index(name) for name in DP + CTX]
        self.ctx = self.z * 8 + self.y * 2 + self.c
        self.dp = self.x * 2 + self.w

    def at_ctx(self, i):
        return (self.x, self.w, i // 8, lax.rem(i // 2, 4), lax.rem(i, 2))

    def at_dp(self, i):
        return (i // 2, lax.rem(i, 2), self.z, self.y, self.c)

    def along_x(self, by):
        return (lax.rem(self.x + by, 4), self.w, self.z, self.y, self.c)

    def along_y(self, by):
        return (self.x, self.w, self.z, lax.rem(self.y + by, 4), self.c)

    def along_z(self, by):
        return (self.x, self.w, lax.rem(self.z + by, 4), self.y, self.c)

    def across_w(self):
        return (self.x, 1 - self.w, self.z, self.y, self.c)

    def across_c(self):
        return (self.x, self.w, self.z, self.y, 1 - self.c)

    def after(self):
        return self.at_ctx(lax.rem(self.ctx + 1, 32))

    def before(self):
        return self.at_ctx(lax.rem(self.ctx + 31, 32))

    def meet(self):
        barrier = pltpu.get_barrier_semaphore()

        @pl.loop(1, 32)
        def _(p):
            place = self.at_ctx(lax.rem(self.ctx + p, 32))
            pl.semaphore_signal(barrier, inc=1, device_id=place, device_id_type=MESH)

        @pl.loop(1, 8)
        def _(p):
            place = self.at_dp(lax.rem(self.dp + p, 8))
            pl.semaphore_signal(barrier, inc=1, device_id=place, device_id_type=MESH)

        pl.semaphore_wait(barrier, 38)


class Links:
    def __init__(self, send, recv, local):
        self.send, self.recv, self.local = send, recv, local

    def to(self, n, place, src, dst):
        return pltpu.make_async_remote_copy(
            src_ref=src, dst_ref=dst, send_sem=self.send.at[n], recv_sem=self.recv.at[n],
            device_id=place, device_id_type=MESH,
        )

    def apart(self, sent, got, place, src, dst):
        return pltpu.make_async_remote_copy(
            src_ref=src, dst_ref=dst, send_sem=self.send.at[sent], recv_sem=self.recv.at[got],
            device_id=place, device_id_type=MESH,
        )

    def own(self, n, src, dst):
        return pltpu.make_async_copy(src, dst, self.local.at[n])

    def pairs(self, base, count, me, place, src, dst, same=False, slot=None, source=None):
        def copy(p):
            peer = lax.rem(me + p, count)
            at = dst.at[slot(peer)] if slot else dst.at[me]
            block = source(peer) if source else src if same else src.at[peer]
            return self.to(base + p, place(peer), block, at)

        def start():
            @pl.loop(1, count)
            def _(p):
                copy(p).start()

        def finish():
            @pl.loop(1, count)
            def _(p):
                copy(p).wait()

        return start, finish


def sems(count):
    return [pltpu.SemaphoreType.DMA((count,)), pltpu.SemaphoreType.DMA((count,)), pltpu.SemaphoreType.DMA((16,))]


def anywhere():
    return pl.BlockSpec(memory_space=pl.ANY)


def comm_call(kernel, name, number, count, out_shape, args, in_specs=None, out_specs=None, scratch=(), room=40):
    return pl.pallas_call(
        kernel,
        out_shape=out_shape,
        in_specs=in_specs or [anywhere()] * len(args),
        out_specs=out_specs or [anywhere()] * len(out_shape),
        scratch_shapes=list(scratch) + sems(count),
        compiler_params=pltpu.CompilerParams(
            collective_id=number, has_side_effects=True, vmem_limit_bytes=room * 1024 * 1024
        ),
        cost_estimate=pl.CostEstimate(flops=10**6, bytes_accessed=2**24, transcendentals=0),
        name=name,
    )(*args)


def b16(*shape):
    return jax.ShapeDtypeStruct(shape, BF16)


def ring_steps(links, here, base, block, out, placed=False, local=7):
    x = here.x
    half = block.shape[0] // 2
    right = links.to(base, here.along_x(1), block, out.at[x])
    left = links.to(base + 1, here.along_x(3), block, out.at[x])
    mine = None if placed else links.own(local, block, out.at[x])
    first = out.at[lax.rem(x + 3, 4), pl.ds(0, half)]
    second = out.at[lax.rem(x + 1, 4), pl.ds(half, half)]
    right_half = links.to(base + 2, here.along_x(1), first, first)
    left_half = links.to(base + 3, here.along_x(3), second, second)

    def begin():
        right.start()
        left.start()
        if mine is not None:
            mine.start()

    def forward():
        right.wait_recv()
        right_half.start()
        left.wait_recv()
        left_half.start()

    def finish():
        right_half.wait()
        left_half.wait()
        right.wait_send()
        left.wait_send()
        if mine is not None:
            mine.wait()

    return begin, forward, finish


def mix_grad_product(own_ref, pair_ref, out_ref, slab, core):
    right = pair_ref[slab, core].reshape(256, 4096)
    cols = pl.ds(pl.multiple_of(slab * 512 + core * 256, 256), 256)
    for part in range(2):
        left = own_ref[2 * part : 2 * part + 2].reshape(256, 4096)
        total = lax.dot_general(left, right, (((1,), (1,)), ((), ())), preferred_element_type=F32)
        out_ref[2 * part : 2 * part + 2, :, cols] = total.astype(BF16).reshape(2, STEP, 256)


def wide_cols(i):
    return pl.ds(pl.multiple_of(i * WIDE, WIDE), WIDE)


def first_kernel(
    grad, weight, filt, streams, taps_ref, masks_ref, first_in, last_in, mid_in, back_in, twist_in,
    stream_out, proj_out, filter_out, tap_out,
    mix_out, filtered_out, early_ref, head_out, mix_next_out, filtered_next_out, prod_next_out, rows_ref, step_ref,
    result_ref, conv_ref, taps_part, tap_first, tap_second, tap_third, row_sum, row_got,
    filt_b, first_ref, last_ref, mid_ref, back_ref, twist_ref,
    own_out, spec_prod, spec_filt, flip_out, grads_out, mixed_out, turned_ref,
    pair_ref, prod_ref, filt_ref, yp_ref, yf_ref, mix_ref, filtered_ref, grads_ref,
    query, head_ref, stage_ref, ext_ref,
    send, recv, local,
):
    here = Here()
    links = Links(send, recv, local)
    x, w, y, c = here.x, here.w, here.y, here.c
    tables = [
        links.own(n, src, dst)
        for n, src, dst in (
            (4, first_in, first_ref), (5, mid_in, mid_ref), (6, twist_in, twist_ref), (12, back_in, back_ref),
            (13, last_in, last_ref),
        )
    ]
    for copy in tables:
        copy.start()
    filt_b[...] = filt[...].astype(BF16)
    here.meet()
    right = links.to(0, here.along_x(1), grad, own_out.at[x])
    left = links.to(1, here.along_x(3), grad, own_out.at[x])
    share = links.to(2, here.across_w(), weight.at[c, y], pair_ref.at[w, c, y])
    prods = links.pairs(16, 32, here.ctx, here.at_ctx, filtered_ref, prod_ref)
    early = links.to(137, here.after(), streams.at[:, pl.ds(112, 16)], early_ref)
    filt_share = links.to(48, here.across_w(), filt_b, filt_ref.at[w, x])
    filt_own = ring_steps(links, here, 184, filt_b, filt_ref.at[w], local=3)
    filt_other = ring_steps(links, here, 188, filt_ref.at[1 - w, x], filt_ref.at[1 - w], placed=True)
    flip = links.to(3, here.across_w(), grad, flip_out.at[x])
    heads = links.to(4, here.before(), head_ref, head_out)
    early.start()
    filt_share.start()
    filt_own[0]()
    share.start()
    right.start()
    left.start()
    locals_ = [
        links.own(0, grad, own_out.at[x]),
        links.own(1, weight, pair_ref.at[w]),
    ]
    for copy in locals_:
        copy.start()
    masks = [masks_ref[:, i : i + 1] for i in range(2)]

    def fetch(i):
        slot = lax.rem(i, 2)
        return links.own(8 + slot, streams.at[:, :, wide_cols(i)], stage_ref.at[slot])

    fetch(0).start()
    early.wait_recv()
    filt_share.wait()
    filt_other[0]()
    filt_own[1]()

    @pl.loop(0, 8)
    def _(i):
        @pl.when(i < 7)
        def _():
            fetch(i + 1).start()

        fetch(i).wait()
        slot, cols = lax.rem(i, 2), wide_cols(i)
        fill_extended(lambda s: stage_ref[slot, s], lambda s: early_ref[s, :, cols], ext_ref)
        taps = lambda t, s: taps_ref[t, s : s + 1, cols]
        query[:, cols] = convolved(ext_ref, taps, masks, 0).astype(BF16)
        key = convolved(ext_ref, taps, masks, 1)
        value = convolved(ext_ref, taps, masks, 2)
        head_ref[0, :, cols] = key[:8]
        head_ref[1, :, cols] = value[:8]
        product = (key * value).astype(BF16)
        for j in range(4):
            filtered_ref[4 * i + j] = product[:, 128 * j : 128 * (j + 1)]

    filt_other[1]()

    def piece(row, part=None):
        ref = pair_ref.at[1 - w, c, row]
        return ref if part is None else ref.at[pl.ds(32 * part, 32)]

    def pass_on(n, place, row, part=None):
        copy = links.to(n, place, piece(row, part), piece(row, part))
        copy.start()
        return copy

    behind, ahead, far = lax.rem(y + 3, 4), lax.rem(y + 1, 4), lax.rem(y + 2, 4)
    share.wait_recv()
    up = pass_on(5, here.along_y(1), y)
    down = pass_on(6, here.along_y(3), y)
    over = [pass_on(7, here.across_c(), y)]
    prods[0]()
    prod_ref[here.ctx] = filtered_ref[here.ctx]
    heads.start()
    up.wait_recv()
    up_half = pass_on(8, here.along_y(1), behind, 0)
    over.append(pass_on(9, here.across_c(), behind))
    down.wait_recv()
    down_half = pass_on(10, here.along_y(3), ahead, 1)
    over.append(pass_on(11, here.across_c(), ahead))
    right.wait_recv()
    half = own_out.at[lax.rem(x + 3, 4), pl.ds(0, 64)]
    right_half = links.to(12, here.along_x(1), half, half)
    right_half.start()
    left.wait_recv()
    half = own_out.at[lax.rem(x + 1, 4), pl.ds(64, 64)]
    left_half = links.to(13, here.along_x(3), half, half)
    left_half.start()
    up_half.wait_recv()
    down_half.wait_recv()
    over.append(pass_on(14, here.across_c(), far))
    filt_own[2]()
    filt_other[2]()
    prods[1]()
    flip.start()
    for copy in locals_:
        copy.wait()

    right_half.wait()
    left_half.wait()
    for copy in over:
        copy.wait()

    @pl.loop(0, 4)
    def _(i):
        mix_grad_product(own_out, pair_ref, mix_ref, i // 2, lax.rem(i, 2))

    for copy in (right, left, share, up, down, up_half, down_half, early):
        copy.wait_send()
    mixes = links.pairs(88, 4, x, lambda i: (i, w, here.z, y, c), mix_ref, mix_out)
    mixes[0]()
    mix_out[x] = mix_ref[x]
    for copy in tables:
        copy.wait()
    filter_forward_kernel(
        prod_ref, filt_ref, first_ref, last_ref, mid_ref, back_ref, twist_ref,
        filtered_ref, spec_prod, spec_filt, yp_ref, yf_ref,
    )
    filtereds = links.pairs(56, 32, here.ctx, here.at_ctx, filtered_ref, filtered_out)
    filtereds[0]()
    filtered_out[here.ctx] = filtered_ref[here.ctx]

    flip.wait()
    ring = ring_steps(links, here, 92, flip_out.at[x], flip_out, placed=True)
    mixes[1]()
    ring[0]()

    @pl.loop(0, 8)
    def _(i):
        mix = mix_out[i // 2, :, wide_cols(lax.rem(i, 2))]
        out = (mix.astype(F32) * query[:, wide_cols(i)].astype(F32)).astype(BF16)
        for j in range(4):
            grads_ref[4 * i + j] = out[:, 128 * j : 128 * (j + 1)]

    grads = links.pairs(96, 32, here.ctx, here.at_ctx, grads_ref, grads_out)
    grads[0]()
    grads_out[here.ctx] = grads_ref[here.ctx]
    mix_next = links.to(15, here.before(), mix_out.at[:, pl.ds(0, 16)], mix_next_out)
    mix_next.start()
    filtereds[1]()

    @pl.loop(0, 8)
    def _(i):
        filtered = jnp.concatenate([filtered_out[4 * i + j] for j in range(4)], 1)
        mixed = (query[:, wide_cols(i)].astype(F32) * filtered.astype(F32)).astype(BF16)
        mix_ref[i // 2, :, wide_cols(lax.rem(i, 2))] = mixed

    mixeds = links.pairs(
        128, 8, here.dp, here.at_dp, None, mixed_out,
        source=lambda peer: mix_ref.at[peer // 2, :, wide_cols(lax.rem(peer, 2))],
        slot=lambda peer: lax.rem(w + lax.rem(peer, 2), 2) * 4 + x,
    )
    mixeds[0]()
    mixed_out[x] = mix_ref[x, :, wide_cols(w)]
    filtered_next = links.to(136, here.before(), filtered_out.at[:, pl.ds(0, 16)], filtered_next_out)
    filtered_next.start()
    ring[1]()
    grads[1]()
    filter_backward_kernel(
        grads_out, spec_prod, spec_filt, first_ref, last_ref, mid_ref, back_ref, twist_ref,
        filtered_ref, grads_ref, yp_ref, yf_ref,
    )
    prod_grads = links.pairs(140, 32, here.ctx, here.at_ctx, filtered_ref, prod_ref)
    prod_grads[0]()
    prod_ref[here.ctx] = filtered_ref[here.ctx]
    mixeds[1]()
    ring[2]()

    @pl.loop(0, 8)
    def _(i):
        at = pl.ds(pl.multiple_of(i * STEP, STEP), STEP)
        turned_ref[:, at] = mixed_out[i].astype(F32).T.astype(BF16)

    @pl.loop(0, 8)
    def _(i):
        cols = wide_cols(i)
        total = dot32(turned_ref[:, :512], own_out[:, :, cols].reshape(512, WIDE))
        total = total + dot32(turned_ref[:, 512:], flip_out[:, :, cols].reshape(512, WIDE))
        total = total.astype(BF16)
        for zz in range(4):
            for yy in range(4):
                for cc in range(2):
                    at = (zz * 8 + yy * 2 + cc) * 16
                    pair_ref[0, cc, yy, 16 * zz : 16 * (zz + 1), cols] = total[at : at + 16]

    half = links.to(138, here.across_c(), pair_ref.at[0, 1 - c], pair_ref.at[1, 0])
    half.start()
    filt_grads = links.pairs(
        172, 8, here.dp, here.at_dp, None, filt_ref, slot=lambda peer: (w, x),
        source=lambda peer: grads_ref.at[pl.ds(4 * peer, 4)]
    )
    filt_grads[0]()
    filt_ref[w, x] = grads_ref[pl.ds(4 * here.dp, 4)]
    half.wait()

    @pl.loop(0, 16)
    def _(i):
        yy = i // 4
        at = pl.ds(pl.multiple_of(lax.rem(i, 4) * 16, 16), 16)
        both = pair_ref[0, c, yy, at, :].astype(F32) + pair_ref[1, 0, yy, at, :].astype(F32)
        pair_ref[1, 1, yy, at, :] = both.astype(BF16)

    up_place, down_place = here.along_y(1), here.along_y(3)
    y_up, y_down, y_far = lax.rem(y + 1, 4), lax.rem(y + 3, 4), lax.rem(y + 2, 4)
    far_steps = [
        links.to(180, up_place, pair_ref.at[1, 1, y_far, pl.ds(0, 32)], step_ref.at[0]),
        links.to(181, down_place, pair_ref.at[1, 1, y_far, pl.ds(32, 32)], step_ref.at[1]),
    ]
    for copy in far_steps:
        copy.start()
    for copy in far_steps:
        copy.wait()
    for side, row in ((0, y_up), (1, y_down)):
        for part in range(2):
            at = pl.ds(32 * side + 16 * part, 16)
            both = pair_ref[1, 1, row, at, :].astype(F32)
            both = both + step_ref[side, 16 * part : 16 * (part + 1), :].astype(F32)
            pair_ref[1, 1, row, at, :] = both.astype(BF16)
    near_steps = [
        links.to(182, up_place, pair_ref.at[1, 1, y_up], rows_ref.at[0]),
        links.to(183, down_place, pair_ref.at[1, 1, y_down], rows_ref.at[1]),
    ]
    for copy in near_steps:
        copy.start()
    prod_grads[1]()
    prod_next = links.to(139, here.before(), prod_ref.at[:, pl.ds(0, 16)], prod_next_out)
    prod_next.start()
    filt_grads[1]()
    total = filt_ref[0, 0].astype(F32)
    for i in range(1, 8):
        total = total + filt_ref[i % 2, i // 2].astype(F32)
    filter_out[...] = total * GRAD_SCALE
    for copy in (heads, mix_next, filtered_next, prod_next):
        copy.wait()
    ahead = [masks_ref[:, 2 + i : 3 + i] for i in range(2)]

    def store(i):
        slot = lax.rem(i, 2)
        return links.own(10 + slot, result_ref.at[slot], stream_out.at[:, :, wide_cols(i)])

    fetch(0).start()

    @pl.loop(0, 8)
    def _(i):
        @pl.when(i < 7)
        def _():
            fetch(i + 1).start()

        @pl.when(i >= 2)
        def _():
            store(i - 2).wait()

        fetch(i).wait()
        slot, cols = lax.rem(i, 2), wide_cols(i)
        mix_cols = wide_cols(lax.rem(i, 2))
        fill_extended(lambda s: stage_ref[slot, s], lambda s: early_ref[s, :, cols], ext_ref)
        taps = lambda t, s: taps_ref[t, s : s + 1, cols]
        key = convolved(ext_ref, taps, masks, 1)
        value = convolved(ext_ref, taps, masks, 2)

        def lanes(ref):
            return jnp.concatenate([ref[4 * i + j] for j in range(4)], 1).astype(F32)

        product_grad = lanes(prod_ref)
        product_next = lanes(prod_next_out)[:2]
        inner, outer = pl.ds(0, STEP), pl.ds(STEP, 2)
        query_grad = mix_out[i // 2, :, mix_cols].astype(F32) * lanes(filtered_out)
        conv_ref[0, inner, :] = query_grad.astype(BF16).astype(F32)
        query_next = mix_next_out[i // 2, :, mix_cols].astype(F32) * lanes(filtered_next_out)
        conv_ref[0, outer, :] = query_next.astype(BF16).astype(F32)[:2]
        conv_ref[1, inner, :] = product_grad * value
        conv_ref[1, outer, :] = product_next * head_out[1, :2, cols]
        conv_ref[2, inner, :] = product_grad * key
        conv_ref[2, outer, :] = product_next * head_out[0, :2, cols]
        for s in range(3):
            at_here = conv_ref[s, inner, :]
            grad_rows = taps(0, s) * at_here
            sums = [jnp.sum(at_here * ext_ref[s, pl.ds(8, STEP), :], axis=0, keepdims=True)]
            for t in (1, 2):
                grad_rows = grad_rows + taps(t, s) * conv_ref[s, pl.ds(t, STEP), :] * ahead[t - 1]
                behind_rows = ext_ref[s, pl.ds(8 - t, STEP), :] * masks[t - 1]
                sums.append(jnp.sum(at_here * behind_rows, axis=0, keepdims=True))
            result_ref[slot, s] = grad_rows.astype(BF16)
            for t in range(3):
                for j in range(4):
                    taps_part[4 * i + j, 3 * t + s : 3 * t + s + 1, :] = sums[t][:, 128 * j : 128 * (j + 1)]
        for j in range(4):
            taps_part[4 * i + j, 9:16, :] = jnp.zeros((7, STEP), F32)
        store(i).start()
        for j in range(4):
            peer = 4 * i + j

            @pl.when(peer != here.ctx)
            def _():
                links.apart(
                    192 + peer, 192 + here.ctx, here.at_ctx(peer), taps_part.at[peer], tap_first.at[here.ctx]
                ).start()

    spread = links.pairs(224, 8, here.dp, here.at_dp, tap_second.at[here.dp], tap_second, same=True)
    gather = links.pairs(232, 32, here.ctx, here.at_ctx, tap_third.at[here.ctx], tap_third, same=True)
    zs = links.pairs(264, 4, here.z, lambda i: (x, w, i, y, c), row_sum, row_got)
    tap_first[here.ctx] = taps_part[here.ctx]
    for copy in near_steps:
        copy.wait()

    @pl.loop(0, 4)
    def _(i):
        at = pl.ds(pl.multiple_of(i * 16, 16), 16)
        total = pair_ref[1, 1, y, at, :].astype(F32)
        for k in range(2):
            total = total + rows_ref[k, at, :].astype(F32)
        row_sum[i] = total.astype(BF16)

    zs[0]()
    row_got[here.z] = row_sum[here.z]

    @pl.loop(1, 32)
    def _(p):
        peer = lax.rem(here.ctx + p, 32)
        links.apart(192 + peer, 192 + peer, here.at_ctx(peer), taps_part.at[peer], tap_first.at[peer]).wait()

    tap_second[here.dp] = jnp.sum(tap_first[...], axis=0)
    spread[0]()
    spread[1]()
    tap_third[here.ctx] = jnp.sum(tap_second[...], axis=0)
    gather[0]()
    zs[1]()
    total = row_got[0].astype(F32)
    for i in range(1, 4):
        total = total + row_got[i].astype(F32)
    proj_out[...] = total * GRAD_SCALE
    store(6).wait()
    store(7).wait()
    gather[1]()
    totals = jnp.concatenate([tap_third[j] for j in range(32)], 1) * GRAD_SCALE
    for t in range(3):
        tap_out[t] = totals[3 * t : 3 * t + 3]


def body(streams, out_grad, proj_weight, long_filter, short_taps, doc_ids):
    rows = streams.shape[1]
    first_row = ((lax.axis_index(DP) * 32) + lax.axis_index(CTX)) * rows
    edge_ids = jnp.full((2,), -1, jnp.int32)
    id_rows = lax.dynamic_slice_in_dim(jnp.concatenate([edge_ids, doc_ids, edge_ids]), first_row, rows + 4)
    own_ids = id_rows[2 : 2 + rows]
    place = lax.axis_index(CTX) * rows + jnp.arange(rows)
    near = [
        jnp.logical_and(id_rows[2 + d : 2 + d + rows] == own_ids, jnp.logical_and(place + d >= 0, place + d < LENGTH))
        for d in (-1, -2, 1, 2)
    ]
    masks = jnp.stack(near + [jnp.zeros((rows,), bool)] * 4, axis=1).astype(F32)
    tables = tables_in()
    block_room = pltpu.VMEM((32, STEP, STEP), BF16)
    spec_room = pltpu.VMEM((SLOTS, 2 * STEP, STEP), F32)
    group_room = pltpu.VMEM((4, rows, 4096), BF16)
    slab_room = pltpu.VMEM((8, rows, WIDE), BF16)
    half_blocks = pltpu.VMEM((32, 16, STEP), BF16)
    part_room = pltpu.VMEM((32, 16, STEP), F32)
    head_room = pltpu.VMEM((2, 8, 4096), F32)
    stage_room = pltpu.VMEM((2, 3, rows, WIDE), BF16)
    ext_room = pltpu.VMEM((3, rows + 8, WIDE), F32)
    mix_room = pltpu.VMEM((4, rows, 1024), BF16)
    row_room = pltpu.VMEM((4, 16, 4096), BF16)
    stream_grads, proj_grad, filter_grad, taps = comm_call(
        first_kernel, "hyena_backward", 1, 268,
        [b16(3, rows, 4096), jax.ShapeDtypeStruct((16, 4096), F32), jax.ShapeDtypeStruct((4, STEP, STEP), F32),
         jax.ShapeDtypeStruct((3, 3, 4096), F32)],
        (out_grad, proj_weight.reshape(2, 4, 64, 4096), long_filter.reshape(4, STEP, STEP), streams,
         short_taps, masks, *tables),
        in_specs=[anywhere()] * 2 + [vmem(), anywhere(), vmem(), vmem()] + [anywhere()] * 5,
        out_specs=[anywhere()] + [vmem()] * 3,
        scratch=[
            mix_room, block_room, pltpu.VMEM((3, 16, 4096), BF16), head_room, pltpu.VMEM((4, 16, 1024), BF16),
            half_blocks, half_blocks, pltpu.VMEM((2, 64, 4096), BF16), pltpu.VMEM((2, 32, 4096), BF16),
            stage_room, ext_room,
            part_room, part_room, pltpu.VMEM((8, 16, STEP), F32), part_room, row_room, row_room,
            pltpu.VMEM((4, STEP, STEP), BF16), *[pltpu.VMEM(table.shape, table.dtype) for table in tables],
            group_room, spec_room, spec_room, group_room, block_room, slab_room, pltpu.VMEM((WIDE, 1024), BF16),
            pltpu.VMEM((2, 2, 4, 64, 4096), BF16), block_room, pltpu.VMEM((2, 4, 4, STEP, STEP), BF16),
            pltpu.VMEM((64, STEP, STEP), F32), pltpu.VMEM((64, STEP, STEP), F32),
            mix_room, block_room, block_room, pltpu.VMEM((rows, 4096), BF16), head_room, stage_room, ext_room,
        ],
        room=62,
    )
    return stream_grads, proj_grad, filter_grad.reshape(512, STEP), taps


def solution(mesh):
    devices = np.asarray(mesh.devices).reshape(4, 2, 4, 4, 2)
    fine = Mesh(devices, ("x", "w", "z", "y", "c"))
    every = DP + CTX
    return jax.shard_map(
        body,
        mesh=fine,
        in_specs=(P(None, every, None), P(every, None), P(DP, None), P(DP, CTX), P(), P()),
        out_specs=(P(None, every, None), P(every, None), P(DP, CTX), P()),
        check_vma=False,
    )
```
